256 devices in a mesh: rep: 32 (over z_hi, x, y), fsdp: 8 (over z_lo, core).
Axes of the slice: x: 4, y: 4, z: 8 (z_hi: 2, z_lo: 4; z = z_hi * 4 + z_lo), core: 2. Of those that a mesh axis runs over, the one named last changes fastest.
Arguments:
- tokens: bfloat16 [98304, 8192], P(('rep', 'fsdp')), may hold values from -6 to 6
- key_weight: bfloat16 [32, 8192, 512], P('rep', 'fsdp'), may hold values from -0.032958984 to 0.032958984
- key_grad: bfloat16 [98304, 512], P(('rep', 'fsdp')), may hold values from -0.099609375 to 0.099609375
- norm_gain: float32 [32, 8192], P('rep'), may hold values from 0.5 to 1.5
- outer_params: float32 [128, 8192], P('fsdp'), may hold values from -6 to 6
- local_params: bfloat16 [32, 128, 8192], P('rep', 'fsdp'), may hold values from -6 to 6
- momentum: float32 [128, 8192], P('fsdp'), may hold values from -6 to 6
- outer_step: int32 [1], replicated, may hold values from 0 to 7
Outputs:
- keys: bfloat16 [98304, 512], P(('rep', 'fsdp'))
- weight_grad: float32 [32, 8192, 512], P('rep', 'fsdp')
- gain_grad: float32 [32, 8192], P('rep')
- new_outer: float32 [128, 8192], P('fsdp')
- new_momentum: float32 [128, 8192], P('fsdp')
The draws below stay inside these ranges and needn't reach their ends.
All inputs are finite; a program needn't handle non-finite values.
Results may differ from the reference program's by a relative error of at most 0.015.
Values may be sent and summed in bfloat16 or wider, within the bound.
A program may use at most 128 MiB of HBM per device.

```python
import jax
import jax.numpy as jnp
from jax import lax

D = 8192
TOK_DEV = 384
WARM = 8
KW = 512
REPS = 32
TOKENS = 98304
FRAG_ROWS = 128
N_REP = 32
N_FSDP = 8


def shard_levels(own_key, shape, split, low, top_value):
    level = 1.0
    for position, blocks in split:
        draws = jax.random.uniform(jax.random.fold_in(jax.random.fold_in(own_key, 6), position), (blocks,), jnp.float32, low / len(split), top_value / len(split))
        level = level * jnp.repeat(jnp.exp(draws), shape[position] // blocks).reshape((-1,) + (1,) * (len(shape) - 1 - position))
    return level


def gaussian(key, extent, deviation, limit, pieces=(), dtype=jnp.bfloat16):
    entries = jax.random.normal(key, extent, jnp.float32) * deviation
    if len(pieces) > 0:
        entries = shard_levels(key, extent, pieces, -0.22, 0.18) * entries
    return jnp.clip(entries, min=-limit, max=limit).astype(dtype)


def setup_inputs(seed: int = 0) -> dict:
    streams_of = jax.random.split(jax.random.key(seed), 9)
    tokens = gaussian(streams_of[0], (TOKENS, D), 1.0, 6.0, ((0, 256),))
    key_weight = gaussian(streams_of[1], (REPS, D, KW), (0.5 * D ** -0.5), 0.032958984, ((0, 32), (1, 8)))
    key_grad = gaussian(streams_of[2], (TOKENS, KW), 0.015, 0.099609375, ((0, 256),))
    norm_gain = jnp.clip(1.0 + 0.1 * jax.random.normal(streams_of[3], (REPS, D), jnp.float32), 0.5, 1.5)
    outer_params = gaussian(streams_of[4], (FRAG_ROWS, D), 1.0, 6.0, ((0, 8),), jnp.float32)
    local_params = gaussian(streams_of[5], (REPS, FRAG_ROWS, D), 1.0, 6.0, ((0, 32), (1, 8)))
    momentum = gaussian(streams_of[6], (FRAG_ROWS, D), 1.0, 6.0, ((0, 8),), jnp.float32)
    outer_step = jax.random.randint(streams_of[7], (1,), 0, WARM).astype(jnp.int32)
    return dict(tokens=tokens, key_weight=key_weight, key_grad=key_grad, norm_gain=norm_gain, outer_params=outer_params, local_params=local_params, momentum=momentum, outer_step=outer_step)


epsilon = 1e-05
OUTER_LR = 0.7
OUTER_MOMENTUM = 0.9

def reference(tokens, key_weight, key_grad, norm_gain, outer_params, local_params, momentum, outer_step):
    groups = tokens.reshape(N_REP, TOK_DEV * N_FSDP, D)
    cotangents = key_grad.reshape(N_REP, TOK_DEV * N_FSDP, KW)

    def one_group(items):
        rows, cotangent, weights, gain = items
        wide = rows.astype(jnp.float32)
        inv_rms = lax.rsqrt(lax.optimization_barrier(jnp.mean(wide * wide, axis=1, keepdims=True)) + epsilon)
        normed = (wide * inv_rms * gain[None, :]).astype(jnp.bfloat16)
        keys_out = jnp.dot(normed, weights, preferred_element_type=jnp.float32).astype(jnp.bfloat16)
        d_normed = jnp.dot(cotangent, weights.T, preferred_element_type=jnp.float32)
        gain_out = lax.optimization_barrier(jnp.sum(d_normed * wide * inv_rms, axis=0))
        blocks_normed = normed.reshape(N_FSDP, TOK_DEV, D)
        blocks_grad = cotangent.reshape(N_FSDP, TOK_DEV, KW)

        def partial_grad(pair):
            return jnp.dot(pair[0].T, pair[1], preferred_element_type=jnp.float32).astype(jnp.bfloat16)
        partials = lax.map(partial_grad, (blocks_normed, blocks_grad))
        weight_out = lax.optimization_barrier(jnp.sum(partials.astype(jnp.float32), axis=0))
        return (keys_out, weight_out, gain_out)
    keys_all, weight_all, gain_all = lax.map(one_group, (groups, cotangents, key_weight, norm_gain))
    pseudo = lax.optimization_barrier(jnp.sum(outer_params[None, :, :] - local_params.astype(jnp.float32), axis=0)) / N_REP
    outer_rate = OUTER_LR * (outer_step[0].astype(jnp.float32) + 1.0) / WARM
    new_momentum = OUTER_MOMENTUM * momentum + pseudo
    new_outer = outer_params - outer_rate * (pseudo + OUTER_MOMENTUM * new_momentum)
    return (keys_all.reshape(TOKENS, KW), weight_all, gain_all, new_outer, new_momentum)
```

```python
import functools

import jax
import jax.numpy as jnp
from jax import lax
from jax.experimental import pallas as pl
from jax.experimental.pallas import tpu as pltpu
from jax.sharding import PartitionSpec as P

MESH = pl.DeviceIdType.MESH
BF16, F32 = jnp.bfloat16, jnp.float32

WARM = 8
EPSILON = 1e-05
OUTER_LR = 0.7
OUTER_MOMENTUM = 0.9

CHIPS, CORES = 4, 2
XS, YS, ZS = 4, 4, 2
CHUNKS = 4
STEPS = CHIPS * CHUNKS
AHEAD = 3
LOADS = 6
ROWS = 16
MIB = 1024 * 1024

W0, P0, S0, R0, L0 = 0, 8, 16, 20, 24
SLOTS = 28


def kernel(
    tok_hbm, kw_hbm, kg_hbm, gain_hbm, op_hbm, lp_hbm, mo_hbm, step_ref,
    keys_hbm, wg_hbm, gg_hbm, no_hbm, nm_hbm,
    tok, nrm, kg, gain, inv, buf, kacc, kout, wg,
    g_own, g_sib, g_z, g_fin,
    xr, ysum, yr, zs, zr, ps, op, mo,
    tok_sem, ld_sem, out_sem,
    r_send, r_recv, l_send, l_recv,
    w_send, w_recv, p_send, p_recv,
    g_send, g_recv, o_send, o_recv,
):
    tokens, width = tok.shape
    shard, kw = buf.shape[1:]
    part = shard // CHUNKS
    frag = op.shape[0]
    xcols, ycols = width // XS, width // XS // YS

    rep, fsdp = lax.axis_index("rep"), lax.axis_index("fsdp")
    q, x, y = rep // (XS * YS), (rep // YS) % XS, rep % YS
    z, c = fsdp // CORES, fsdp % CORES
    o = 1 - c

    def at_rep(q_, x_, y_):
        return ((q_ * XS + x_) * YS + y_, fsdp)

    def at_chip(z_):
        return (rep, z_ * CORES + c)

    sibling = (rep, z * CORES + o)
    right, left = at_chip(lax.rem(z + 1, CHIPS)), at_chip(lax.rem(z + CHIPS - 1, CHIPS))
    has_right, has_left = z < CHIPS - 1, z > 0

    def remote(src, dst, send, recv, device):
        return pltpu.make_async_remote_copy(
            src_ref=src, dst_ref=dst, send_sem=send, recv_sem=recv, device_id=device, device_id_type=MESH
        )

    def rows_of(i):
        return pl.ds(pl.multiple_of(i * part, part), part)

    block = tokens // LOADS

    def tok_load(b):
        rows = pl.ds(pl.multiple_of(b * block, block), block)
        return pltpu.make_async_copy(tok_hbm.at[rows], tok.at[rows], tok_sem.at[b])

    load_gain = pltpu.make_async_copy(gain_hbm, gain, ld_sem.at[0])
    load_kg = pltpu.make_async_copy(kg_hbm, kg, ld_sem.at[1])
    load_w = pltpu.make_async_copy(kw_hbm, buf.at[W0 + 2 * z + c], ld_sem.at[2])
    own_x = pl.ds(pl.multiple_of(x * xcols, xcols), xcols)
    load_lp = pltpu.make_async_copy(lp_hbm.at[:, own_x], xr.at[x], ld_sem.at[3])
    load_op = pltpu.make_async_copy(op_hbm, op, ld_sem.at[4])
    load_mo = pltpu.make_async_copy(mo_hbm, mo, ld_sem.at[5])

    load_gain.start()
    tok_load(0).start()
    load_kg.start()
    for b in range(1, LOADS):
        tok_load(b).start()
    for load in (load_w, load_lp, load_op, load_mo):
        load.start()

    barrier = pltpu.get_barrier_semaphore()
    peers = [at_chip(lax.rem(z + d, CHIPS)) for d in range(1, CHIPS)] + [sibling]
    peers += [at_rep(q, lax.rem(x + d, XS), y) for d in range(1, XS)]
    peers += [at_rep(q, x, lax.rem(y + d, YS)) for d in range(1, YS)]
    peers += [at_rep(1 - q, x, y)]
    for peer in peers:
        pl.semaphore_signal(barrier, inc=1, device_id=peer, device_id_type=MESH)
    pl.semaphore_wait(barrier, len(peers))

    def line_first(n, rightward):
        rows = rows_of(n)
        dst = buf.at[W0 + 2 * z + c, rows]
        if rightward:
            return remote(kw_hbm.at[rows], dst, r_send.at[n], r_recv.at[n], right)
        return remote(kw_hbm.at[rows], dst, l_send.at[n], l_recv.at[n], left)

    def line_copy(n, rightward):
        k, rows = n // CHUNKS, rows_of(n % CHUNKS)
        if rightward:
            is_sum = (k - z + CHIPS - 1) // CHIPS
            weight, owner = 2 * (z - k) + c, CHIPS + z - k
            src = (1 - is_sum) * (W0 + weight) + is_sum * (P0 + 2 * owner + c)
            dst = (1 - is_sum) * (W0 + weight) + is_sum * (R0 + owner)
            return remote(buf.at[src, rows], buf.at[dst, rows], r_send.at[n], r_recv.at[n], right)
        is_sum = (k + z) // CHIPS
        weight, owner = 2 * (z + k) + c, k + z - CHIPS
        src = (1 - is_sum) * (W0 + weight) + is_sum * (P0 + 2 * owner + c)
        dst = (1 - is_sum) * (W0 + weight) + is_sum * (L0 + owner)
        return remote(buf.at[src, rows], buf.at[dst, rows], l_send.at[n], l_recv.at[n], left)

    for n in range(CHUNKS):

        @pl.when(has_right)
        def _():
            line_first(n, True).start()

        @pl.when(has_left)
        def _():
            line_first(n, False).start()

    def own_to_sibling(i):
        rows = rows_of(i)
        return remote(
            kw_hbm.at[rows], buf.at[W0 + 2 * z + c, rows], w_send.at[z, i], w_recv.at[z, i], sibling
        )

    def to_sibling(a, i):
        there = buf.at[W0 + 2 * a + c, rows_of(i)]
        return remote(there, there, w_send.at[a, i], w_recv.at[a, i], sibling)

    def from_sibling(a, i):
        there = buf.at[W0 + 2 * a + o, rows_of(i)]
        return remote(there, there, w_send.at[a, i], w_recv.at[a, i], sibling)

    def terms_to_sibling(j, i):
        return remote(
            buf.at[P0 + 2 * j + o, rows_of(i)], buf.at[S0 + j, rows_of(i)], p_send.at[j, i], p_recv.at[j, i], sibling
        )

    for i in range(CHUNKS):
        own_to_sibling(i).start()

    def x_copy(d):
        to = lax.rem(x + d, XS)
        cols = pl.ds(pl.multiple_of(to * xcols, xcols), xcols)
        return remote(lp_hbm.at[:, cols], xr.at[x], o_send.at[0, d - 1], o_recv.at[0, d - 1], at_rep(q, to, y))

    def x_wait(d):
        slot = xr.at[lax.rem(x + XS - d, XS)]
        return remote(slot, slot, o_send.at[0, d - 1], o_recv.at[0, d - 1], sibling)

    def y_copy(d):
        to = lax.rem(y + d, YS)
        return remote(ysum.at[to], yr.at[y], o_send.at[1, d - 1], o_recv.at[1, d - 1], at_rep(q, x, to))

    def y_wait(d):
        slot = yr.at[lax.rem(y + YS - d, YS)]
        return remote(slot, slot, o_send.at[1, d - 1], o_recv.at[1, d - 1], sibling)

    z_copy = remote(zs, zr, o_send.at[2, 0], o_recv.at[2, 0], at_rep(1 - q, x, y))

    def y_back(d):
        piece = ps.at[x, y]
        return remote(
            piece, piece, o_send.at[3, d - 1], o_recv.at[3, d - 1], at_rep(q, x, lax.rem(y + d, YS))
        )

    def y_back_wait(d):
        piece = ps.at[x, lax.rem(y + YS - d, YS)]
        return remote(piece, piece, o_send.at[3, d - 1], o_recv.at[3, d - 1], sibling)

    def x_back(d):
        piece = ps.at[x]
        return remote(
            piece, piece, o_send.at[4, d - 1], o_recv.at[4, d - 1], at_rep(q, lax.rem(x + d, XS), y)
        )

    def x_back_wait(d):
        piece = ps.at[lax.rem(x + XS - d, XS)]
        return remote(piece, piece, o_send.at[4, d - 1], o_recv.at[4, d - 1], sibling)

    for d in range(1, XS):
        x_copy(d).start()

    load_gain.wait()
    lanes = 128
    pieces = width // lanes

    @pl.loop(0, LOADS)
    def _(b):
        tok_load(b).wait()

        @pl.loop(0, block // ROWS)
        def _(r):
            rows = pl.ds(pl.multiple_of(b * block + r * ROWS, ROWS), ROWS)
            sums = [jnp.zeros((ROWS, lanes), F32) for _ in range(4)]
            for m in range(pieces):
                wide = tok[rows, m * lanes : (m + 1) * lanes].astype(F32)
                sums[m % 4] = sums[m % 4] + wide * wide
            total = jnp.sum((sums[0] + sums[1]) + (sums[2] + sums[3]), axis=1, keepdims=True)
            scale = jnp.broadcast_to(lax.rsqrt(total * (1.0 / width) + EPSILON), (ROWS, lanes))
            inv[rows, :] = scale
            for m in range(pieces):
                cols = slice(m * lanes, (m + 1) * lanes)
                nrm[rows, cols] = (tok[rows, cols].astype(F32) * scale * gain[:, cols]).astype(BF16)

    load_kg.wait()
    upper = z // (CHIPS // 2)

    def cols_of(owner, i):
        return pl.ds(pl.multiple_of(owner * shard + i * part, part), part)

    def terms(owner, i):
        got = lax.dot_general(
            nrm[:, cols_of(owner, i)], kg[...], (((0,), (0,)), ((), ())), preferred_element_type=F32
        )
        buf[P0 + owner, rows_of(i), :] = got.astype(BF16)

    @pl.loop(0, STEPS)
    def _(t):
        n, i = t // CHUNKS, t % CHUNKS
        j = (1 - upper) * (CHIPS - 1 - n) + upper * n
        terms(2 * j + o, i)
        terms_to_sibling(j, i).start()
        terms(2 * j + c, i)

    kacc[...] = jnp.zeros_like(kacc)
    load_w.wait()

    def use_rows(a, core, i):
        owner = 2 * a + core
        rows = buf[W0 + owner, rows_of(i), :]
        cols = cols_of(owner, i)
        kacc[...] += jnp.dot(nrm[:, cols], rows, preferred_element_type=F32)
        d_normed = lax.dot_general(kg[...], rows, (((1,), (1,)), ((), ())), preferred_element_type=F32)
        wide = tok[:, cols].astype(F32)
        for m in range(part // lanes):
            here = slice(m * lanes, (m + 1) * lanes)
            got = jnp.sum(d_normed[:, here] * wide[:, here] * inv[...], axis=0, keepdims=True)
            g_own[core, a, pl.ds(i * (part // lanes) + m, 1), :] = got

    def use_both(a, i):
        use_rows(a, c, i)
        from_sibling(a, i).wait_recv()
        use_rows(a, o, i)

    def add_terms(j, i, base, from_line):
        rows = rows_of(i)
        terms_to_sibling(j, i).wait_recv()
        own = buf[P0 + 2 * j + c, rows, :].astype(F32) + buf[S0 + j, rows, :].astype(F32)

        @pl.when(from_line)
        def _():
            buf[P0 + 2 * j + c, rows, :] = (own + buf[base + j, rows, :].astype(F32)).astype(BF16)

        @pl.when(jnp.logical_not(from_line))
        def _():
            buf[P0 + 2 * j + c, rows, :] = own.astype(BF16)

    def write_rows(i):
        rows = rows_of(i)
        return pltpu.make_async_copy(wg.at[rows], wg_hbm.at[rows], out_sem.at[i])

    write_keys = pltpu.make_async_copy(kout, keys_hbm, out_sem.at[CHUNKS])
    write_gain = pltpu.make_async_copy(g_fin, gg_hbm, out_sem.at[CHUNKS + 1])
    write_op = pltpu.make_async_copy(op, no_hbm, out_sem.at[CHUNKS + 2])
    write_mo = pltpu.make_async_copy(mo, nm_hbm, out_sem.at[CHUNKS + 3])

    gain_swap = remote(g_own.at[o], g_sib, g_send.at[0], g_recv.at[0], sibling)

    def gain_copy(d):
        return remote(g_z.at[z], g_z.at[z], g_send.at[d], g_recv.at[d], at_chip(lax.rem(z + d, CHIPS)))

    def gain_wait(d):
        slot = g_z.at[lax.rem(z + CHIPS - d, CHIPS)]
        return remote(slot, slot, g_send.at[d], g_recv.at[d], sibling)

    gain_back = remote(g_fin.at[:, c], g_fin.at[:, c], g_send.at[CHIPS], g_recv.at[CHIPS], sibling)

    @pl.loop(0, STEPS)
    def _(s):
        k, i = s // CHUNKS, s % CHUNKS

        @pl.when(s == 2)
        def _():
            load_lp.wait()
            for d in range(1, XS):
                x_wait(d).wait_recv()
            for m in range(YS):
                cols = slice(m * ycols, (m + 1) * ycols)
                ysum[m] = (xr[0, :, cols].astype(F32) + xr[1, :, cols].astype(F32)) + (
                    xr[2, :, cols].astype(F32) + xr[3, :, cols].astype(F32)
                )
            for d in range(1, YS):
                y_copy(d).start()
            yr[y] = ysum[y]

        @pl.when(s == 3)
        def _():
            for d in range(1, YS):
                y_wait(d).wait_recv()
            load_op.wait()
            cols = pl.ds(pl.multiple_of(x * xcols + y * ycols, ycols), ycols)
            total = (yr[0] + yr[1]) + (yr[2] + yr[3])
            zs[...] = (float(XS * YS) * op[:, cols] - total).astype(BF16)
            z_copy.start()

        @pl.when(s == 8)
        def _():
            z_copy.wait_recv()
            ps[x, y] = (zs[...].astype(F32) + zr[...].astype(F32)) * (1.0 / (XS * YS * ZS))
            for d in range(1, YS):
                y_back(d).start()

        @pl.when(s == 9)
        def _():
            for d in range(1, YS):
                y_back_wait(d).wait_recv()
            for d in range(1, XS):
                x_back(d).start()

        @pl.when(s == 10)
        def _():
            for d in range(1, XS):
                x_back_wait(d).wait_recv()
            load_mo.wait()
            rate = OUTER_LR * (step_ref[0].astype(F32) + 1.0) / WARM
            for a in range(XS):
                for b in range(YS):
                    cols = slice((a * YS + b) * ycols, (a * YS + b + 1) * ycols)
                    pseudo = ps[a, b]
                    moment = OUTER_MOMENTUM * mo[:, cols] + pseudo
                    mo[:, cols] = moment
                    op[:, cols] = op[:, cols] - rate * (pseudo + OUTER_MOMENTUM * moment)
            write_op.start()
            write_mo.start()

        @pl.when(s == STEPS - 1)
        def _():
            for d in range(1, CHIPS):
                gain_wait(d).wait_recv()
            g_fin[:, c] = (g_z[0] + g_z[1]) + (g_z[2] + g_z[3])
            gain_back.start()

        @pl.when(has_left)
        def _():
            line_copy(s, True).wait_recv()

        @pl.when(has_right)
        def _():
            line_copy(s, False).wait_recv()

        left_weights = jnp.logical_and(has_left, k <= z - 1)
        right_weights = jnp.logical_and(has_right, k <= CHIPS - 2 - z)

        @pl.when(left_weights)
        def _():
            to_sibling(z - 1 - k, i).start()

        @pl.when(right_weights)
        def _():
            to_sibling(z + 1 + k, i).start()

        later = k + 1

        @pl.when(jnp.logical_and(has_right, jnp.logical_and(later < CHIPS, later > z)))
        def _():
            add_terms(CHIPS + z - later, i, R0, has_left)

        @pl.when(jnp.logical_and(has_left, jnp.logical_and(later < CHIPS, later > CHIPS - 1 - z)))
        def _():
            add_terms(later + z - CHIPS, i, L0, has_right)

        n = s + AHEAD

        @pl.when(jnp.logical_and(has_right, jnp.logical_and(n >= CHUNKS, n < STEPS)))
        def _():
            line_copy(n, True).start()

        @pl.when(jnp.logical_and(has_left, jnp.logical_and(n >= CHUNKS, n < STEPS)))
        def _():
            line_copy(n, False).start()

        @pl.when(k == CHIPS - 1)
        def _():
            rows = rows_of(i)
            terms_to_sibling(z, i).wait_recv()
            wg[rows, :] = buf[P0 + 2 * z + c, rows, :].astype(F32) + buf[S0 + z, rows, :].astype(F32)

            @pl.when(has_left)
            def _():
                wg[rows, :] += buf[R0 + z, rows, :].astype(F32)

            @pl.when(has_right)
            def _():
                wg[rows, :] += buf[L0 + z, rows, :].astype(F32)

            write_rows(i).start()

        before = s - 1 + CHUNKS
        k_before, i_before = before // CHUNKS - 1, before % CHUNKS

        @pl.when(jnp.logical_and(s > 0, jnp.logical_and(has_left, k_before <= z - 1)))
        def _():
            use_both(z - 1 - k_before, i_before)

        @pl.when(jnp.logical_and(s > 0, jnp.logical_and(has_right, k_before <= CHIPS - 2 - z)))
        def _():
            use_both(z + 1 + k_before, i_before)

        @pl.when(k == 1)
        def _():
            use_both(z, i)

        @pl.when(s == STEPS - CHUNKS)
        def _():
            gain_swap.start()
            gain_swap.wait_recv()
            g_z[z] = g_own[c] + g_sib[...]
            for d in range(1, CHIPS):
                gain_copy(d).start()
            kout[...] = kacc[...].astype(BF16)
            write_keys.start()

    gain_back_in = remote(g_fin.at[:, o], g_fin.at[:, o], g_send.at[CHIPS], g_recv.at[CHIPS], sibling)
    gain_back_in.wait_recv()
    write_gain.start()

    @pl.when(has_right)
    def _():
        @pl.loop(0, STEPS)
        def _(n):
            line_copy(n, True).wait_send()

    @pl.when(has_left)
    def _():
        @pl.loop(0, STEPS)
        def _(n):
            line_copy(n, False).wait_send()

    @pl.loop(0, STEPS)
    def _(t):
        to_sibling(t // CHUNKS, t % CHUNKS).wait_send()
        terms_to_sibling(t // CHUNKS, t % CHUNKS).wait_send()

    gain_swap.wait_send()
    gain_back.wait_send()
    for d in range(1, CHIPS):
        gain_copy(d).wait_send()
    for d in range(1, XS):
        x_copy(d).wait_send()
        x_back(d).wait_send()
    for d in range(1, YS):
        y_copy(d).wait_send()
        y_back(d).wait_send()
    z_copy.wait_send()

    for i in range(CHUNKS):
        write_rows(i).wait()
    for write in (write_keys, write_gain, write_op, write_mo):
        write.wait()


def local(tokens, key_weight, key_grad, norm_gain, outer_params, local_params, momentum, outer_step):
    rows, width = tokens.shape
    _, shard, kw = key_weight.shape
    frag = outer_params.shape[0]
    xcols, ycols = width // XS, width // XS // YS
    lanes = 128
    dma, anywhere = pltpu.SemaphoreType.DMA, pl.BlockSpec(memory_space=pl.ANY)
    keys, weight_grad, gain_grad, new_outer, new_momentum = pl.pallas_call(
        kernel,
        out_shape=(
            jax.ShapeDtypeStruct((rows, kw), BF16),
            jax.ShapeDtypeStruct((shard, kw), F32),
            jax.ShapeDtypeStruct((CHIPS, CORES, shard // lanes, lanes), F32),
            jax.ShapeDtypeStruct(outer_params.shape, F32),
            jax.ShapeDtypeStruct(momentum.shape, F32),
        ),
        in_specs=[anywhere] * 7 + [pl.BlockSpec(memory_space=pltpu.SMEM)],
        out_specs=(anywhere,) * 5,
        scratch_shapes=[
            pltpu.VMEM((rows, width), BF16),
            pltpu.VMEM((rows, width), BF16),
            pltpu.VMEM((rows, kw), BF16),
            pltpu.VMEM((1, width), F32),
            pltpu.VMEM((rows, lanes), F32),
            pltpu.VMEM((SLOTS, shard, kw), BF16),
            pltpu.VMEM((rows, kw), F32),
            pltpu.VMEM((rows, kw), BF16),
            pltpu.VMEM((shard, kw), F32),
            pltpu.VMEM((CORES, CHIPS, shard // lanes, lanes), F32),
            pltpu.VMEM((CHIPS, shard // lanes, lanes), F32),
            pltpu.VMEM((CHIPS, CHIPS, shard // lanes, lanes), F32),
            pltpu.VMEM((CHIPS, CORES, shard // lanes, lanes), F32),
            pltpu.VMEM((XS, frag, xcols), BF16),
            pltpu.VMEM((YS, frag, ycols), F32),
            pltpu.VMEM((YS, frag, ycols), F32),
            pltpu.VMEM((frag, ycols), BF16),
            pltpu.VMEM((frag, ycols), BF16),
            pltpu.VMEM((XS, YS, frag, ycols), F32),
            pltpu.VMEM((frag, width), F32),
            pltpu.VMEM((frag, width), F32),
            dma((LOADS,)),
            dma((6,)),
            dma((CHUNKS + 4,)),
            dma((STEPS,)),
            dma((STEPS,)),
            dma((STEPS,)),
            dma((STEPS,)),
            dma((CHIPS, CHUNKS)),
            dma((CHIPS, CHUNKS)),
            dma((CHIPS, CHUNKS)),
            dma((CHIPS, CHUNKS)),
            dma((CHIPS + 1,)),
            dma((CHIPS + 1,)),
            dma((5, 3)),
            dma((5, 3)),
        ],
        compiler_params=pltpu.CompilerParams(
            collective_id=0, has_side_effects=True, vmem_limit_bytes=60 * MIB
        ),
        cost_estimate=pl.CostEstimate(
            flops=6 * rows * width * kw, bytes_accessed=16 * MIB, transcendentals=rows
        ),
        name="outer_and_keys",
    )(
        tokens, key_weight[0], key_grad, norm_gain, outer_params, local_params[0], momentum, outer_step
    )
    return keys, weight_grad[None], gain_grad.reshape(1, width), new_outer, new_momentum


def solution(mesh):
    placed = (
        P(("rep", "fsdp"), None),
        P("rep", "fsdp", None),
        P(("rep", "fsdp"), None),
        P("rep", None),
        P("fsdp", None),
        P("rep", "fsdp", None),
        P("fsdp", None),
        P(),
    )
    return jax.shard_map(
        local,
        mesh=mesh,
        in_specs=placed,
        out_specs=(
            P(("rep", "fsdp"), None),
            P("rep", "fsdp", None),
            P("rep", None),
            P("fsdp", None),
            P("fsdp", None),
        ),
        check_vma=False,
    )
```

```python
import functools

import jax
import jax.numpy as jnp
from jax import lax
from jax.experimental import pallas as pl
from jax.experimental.pallas import tpu as pltpu
from jax.sharding import PartitionSpec as P

MESH = pl.DeviceIdType.MESH
BF16, F32 = jnp.bfloat16, jnp.float32

WARM = 8
EPSILON = 1e-05
OUTER_LR = 0.7
OUTER_MOMENTUM = 0.9

CHIPS, CORES = 4, 2
XS, YS, ZS = 4, 4, 2
CHUNKS = 4
STEPS = CHIPS * CHUNKS
LAST = STEPS - CHUNKS
LOADS = 6
ROWS = 16
MIB = 1024 * 1024

W0, P0, S0, R0, L0 = 0, 8, 16, 20, 24
SLOTS = 28


def kernel(
    tok_hbm, kw_hbm, kg_hbm, gain_hbm, op_hbm, lp_hbm, mo_hbm, step_ref,
    kout, wg, g_fin, op, mo,
    tok, nrm, kg, gain, inv, buf, kacc,
    g_own, g_sib, g_z,
    xr, ysum, yr, zs, zr, ps,
    tok_sem, ld_sem,
    r_send, r_recv, l_send, l_recv,
    w_send, w_recv, p_send, p_recv,
    g_send, g_recv, o_send, o_recv, here_sem,
):
    tokens, width = tok.shape
    shard, kw = buf.shape[1:]
    part = shard // CHUNKS
    frag = op.shape[0]
    xcols, ycols = width // XS, width // XS // YS

    rep, fsdp = lax.axis_index("rep"), lax.axis_index("fsdp")
    q, x, y = rep // (XS * YS), (rep // YS) % XS, rep % YS
    z, c = fsdp // CORES, fsdp % CORES
    o = 1 - c

    def at_rep(q_, x_, y_):
        return ((q_ * XS + x_) * YS + y_, fsdp)

    def at_chip(z_):
        return (rep, z_ * CORES + c)

    sibling = (rep, z * CORES + o)
    right, left = at_chip(lax.rem(z + 1, CHIPS)), at_chip(lax.rem(z + CHIPS - 1, CHIPS))
    has_right, has_left = z < CHIPS - 1, z > 0

    def remote(src, dst, send, recv, device):
        return pltpu.make_async_remote_copy(
            src_ref=src, dst_ref=dst, send_sem=send, recv_sem=recv, device_id=device, device_id_type=MESH
        )

    def rows_of(i):
        return pl.ds(pl.multiple_of(i * part, part), part)

    barrier = pltpu.get_barrier_semaphore()
    partner = at_rep(1 - q, x, y)
    peers = [sibling]
    peers += [at_rep(q, lax.rem(x + d, XS), y) for d in range(1, XS)]
    peers += [at_rep(q, x, lax.rem(y + d, YS)) for d in range(1, YS)]

    def greet(peer):
        pl.semaphore_signal(barrier, inc=1, device_id=peer, device_id_type=MESH)

    @pl.when(has_right)
    def _():
        greet(right)

    @pl.when(has_left)
    def _():
        greet(left)

    for peer in peers:
        greet(peer)

    @pl.when(q == 0)
    def _():
        greet(partner)

    block = tokens // LOADS

    def tok_load(b):
        rows = pl.ds(pl.multiple_of(b * block, block), block)
        return pltpu.make_async_copy(tok_hbm.at[rows], tok.at[rows], tok_sem.at[b])

    load_gain = pltpu.make_async_copy(gain_hbm, gain, ld_sem.at[0])
    load_kg = pltpu.make_async_copy(kg_hbm, kg, ld_sem.at[1])
    load_w = pltpu.make_async_copy(kw_hbm, buf.at[W0 + 2 * z + c], ld_sem.at[2])
    own_x = pl.ds(pl.multiple_of(x * xcols, xcols), xcols)
    load_lp = pltpu.make_async_copy(lp_hbm.at[:, own_x], xr.at[x], ld_sem.at[3])
    load_op = pltpu.make_async_copy(op_hbm, op, ld_sem.at[4])
    load_mo = pltpu.make_async_copy(mo_hbm, mo, ld_sem.at[5])

    load_gain.start()
    tok_load(0).start()
    load_kg.start()
    for b in range(1, LOADS):
        tok_load(b).start()
    for load in (load_w, load_lp, load_op, load_mo):
        load.start()

    middle = jnp.logical_and(has_left, has_right).astype(jnp.int32)
    pl.semaphore_wait(barrier, len(peers) + 1 + middle + q)

    def line_first(n, rightward):
        rows = rows_of(n)
        dst = buf.at[W0 + 2 * z + c, rows]
        if rightward:
            return remote(kw_hbm.at[rows], dst, r_send.at[n], r_recv.at[n], right)
        return remote(kw_hbm.at[rows], dst, l_send.at[n], l_recv.at[n], left)

    def line_copy(n, rightward):
        k, rows = n // CHUNKS, rows_of(n % CHUNKS)
        if rightward:
            is_sum = (k - z + CHIPS - 1) // CHIPS
            weight, owner = 2 * (z - k) + c, CHIPS + z - k
            src = (1 - is_sum) * (W0 + weight) + is_sum * (P0 + 2 * owner + c)
            dst = (1 - is_sum) * (W0 + weight) + is_sum * (R0 + owner)
            return remote(buf.at[src, rows], buf.at[dst, rows], r_send.at[n], r_recv.at[n], right)
        is_sum = (k + z) // CHIPS
        weight, owner = 2 * (z + k) + c, k + z - CHIPS
        src = (1 - is_sum) * (W0 + weight) + is_sum * (P0 + 2 * owner + c)
        dst = (1 - is_sum) * (W0 + weight) + is_sum * (L0 + owner)
        return remote(buf.at[src, rows], buf.at[dst, rows], l_send.at[n], l_recv.at[n], left)

    for n in range(CHUNKS):

        @pl.when(has_right)
        def _():
            line_first(n, True).start()

        @pl.when(has_left)
        def _():
            line_first(n, False).start()

    def own_to_sibling(i):
        rows = rows_of(i)
        return remote(
            kw_hbm.at[rows], buf.at[W0 + 2 * z + c, rows], w_send.at[z, i], w_recv.at[z, i], sibling
        )

    def to_sibling(a, i):
        there = buf.at[W0 + 2 * a + c, rows_of(i)]
        return remote(there, there, w_send.at[a, i], w_recv.at[a, i], sibling)

    def from_sibling(a, i):
        there = buf.at[W0 + 2 * a + o, rows_of(i)]
        return remote(there, there, w_send.at[a, i], w_recv.at[a, i], sibling)

    def terms_to_sibling(j, i):
        return remote(
            buf.at[P0 + 2 * j + o, rows_of(i)], buf.at[S0 + j, rows_of(i)], p_send.at[j, i], p_recv.at[j, i], sibling
        )

    for i in range(CHUNKS):
        own_to_sibling(i).start()

    def x_copy(d):
        to = lax.rem(x + d, XS)
        cols = pl.ds(pl.multiple_of(to * xcols, xcols), xcols)
        return remote(lp_hbm.at[:, cols], xr.at[x], o_send.at[0, d - 1], o_recv.at[0, d - 1], at_rep(q, to, y))

    def x_wait(d):
        slot = xr.at[lax.rem(x + XS - d, XS)]
        return remote(slot, slot, o_send.at[0, d - 1], o_recv.at[0, d - 1], sibling)

    def y_copy(d):
        to = lax.rem(y + d, YS)
        return remote(ysum.at[to], yr.at[y], o_send.at[1, d - 1], o_recv.at[1, d - 1], at_rep(q, x, to))

    def y_wait(d):
        slot = yr.at[lax.rem(y + YS - d, YS)]
        return remote(slot, slot, o_send.at[1, d - 1], o_recv.at[1, d - 1], sibling)

    z_copy = remote(zs, zr, o_send.at[2, 0], o_recv.at[2, 0], partner)

    def y_back(d):
        piece = ps.at[x, y]
        return remote(
            piece, piece, o_send.at[3, d - 1], o_recv.at[3, d - 1], at_rep(q, x, lax.rem(y + d, YS))
        )

    def y_back_wait(d):
        piece = ps.at[x, lax.rem(y + YS - d, YS)]
        return remote(piece, piece, o_send.at[3, d - 1], o_recv.at[3, d - 1], sibling)

    def x_back(d):
        piece = ps.at[x]
        return remote(
            piece, piece, o_send.at[4, d - 1], o_recv.at[4, d - 1], at_rep(q, lax.rem(x + d, XS), y)
        )

    def x_back_wait(d):
        piece = ps.at[lax.rem(x + XS - d, XS)]
        return remote(piece, piece, o_send.at[4, d - 1], o_recv.at[4, d - 1], sibling)

    for d in range(1, XS):
        x_copy(d).start()

    @pl.when(q == 1)
    def _():
        pl.semaphore_signal(here_sem, inc=1, device_id=partner, device_id_type=MESH)

    load_gain.wait()
    lanes = 128
    pieces = width // lanes

    @pl.loop(0, LOADS)
    def _(b):
        tok_load(b).wait()

        @pl.loop(0, block // ROWS)
        def _(r):
            rows = pl.ds(pl.multiple_of(b * block + r * ROWS, ROWS), ROWS)
            sums = [jnp.zeros((ROWS, lanes), F32) for _ in range(4)]
            for m in range(pieces):
                wide = tok[rows, m * lanes : (m + 1) * lanes].astype(F32)
                sums[m % 4] = sums[m % 4] + wide * wide
            total = jnp.sum((sums[0] + sums[1]) + (sums[2] + sums[3]), axis=1, keepdims=True)
            scale = jnp.broadcast_to(lax.rsqrt(total * (1.0 / width) + EPSILON), (ROWS, lanes))
            inv[rows, :] = scale
            for m in range(pieces):
                cols = slice(m * lanes, (m + 1) * lanes)
                nrm[rows, cols] = (tok[rows, cols].astype(F32) * scale * gain[:, cols]).astype(BF16)

    load_kg.wait()
    upper = z // (CHIPS // 2)

    def cols_of(owner, i):
        return pl.ds(pl.multiple_of(owner * shard + i * part, part), part)

    def terms(owner, i):
        got = lax.dot_general(
            nrm[:, cols_of(owner, i)], kg[...], (((0,), (0,)), ((), ())), preferred_element_type=F32
        )
        buf[P0 + owner, rows_of(i), :] = got.astype(BF16)

    @pl.loop(0, STEPS)
    def _(t):
        n, i = t // CHUNKS, t % CHUNKS
        j = (1 - upper) * (CHIPS - 1 - n) + upper * n
        terms(2 * j + o, i)
        terms_to_sibling(j, i).start()
        terms(2 * j + c, i)

    kacc[...] = jnp.zeros_like(kacc)
    load_w.wait()

    def use_rows(a, core, i):
        owner = 2 * a + core
        rows = buf[W0 + owner, rows_of(i), :]
        cols = cols_of(owner, i)
        kacc[...] += jnp.dot(nrm[:, cols], rows, preferred_element_type=F32)
        d_normed = lax.dot_general(kg[...], rows, (((1,), (1,)), ((), ())), preferred_element_type=F32)
        wide = tok[:, cols].astype(F32)
        for m in range(part // lanes):
            here = slice(m * lanes, (m + 1) * lanes)
            got = jnp.sum(d_normed[:, here] * wide[:, here] * inv[...], axis=0, keepdims=True)
            g_own[core, a, pl.ds(i * (part // lanes) + m, 1), :] = got

    def use_both(a, i):
        use_rows(a, c, i)
        from_sibling(a, i).wait_recv()
        use_rows(a, o, i)

    def add_terms(j, i, base, from_line):
        rows = rows_of(i)
        terms_to_sibling(j, i).wait_recv()
        own = buf[P0 + 2 * j + c, rows, :].astype(F32) + buf[S0 + j, rows, :].astype(F32)

        @pl.when(from_line)
        def _():
            buf[P0 + 2 * j + c, rows, :] = (own + buf[base + j, rows, :].astype(F32)).astype(BF16)

        @pl.when(jnp.logical_not(from_line))
        def _():
            buf[P0 + 2 * j + c, rows, :] = own.astype(BF16)

    gain_swap = remote(g_own.at[o], g_sib, g_send.at[0], g_recv.at[0], sibling)

    def gain_copy(d):
        to = lax.rem(z + d, CHIPS)
        return remote(g_own.at[c, to], g_z.at[z], g_send.at[d], g_recv.at[d], at_chip(to))

    def gain_wait(d):
        slot = g_z.at[lax.rem(z + CHIPS - d, CHIPS)]
        return remote(slot, slot, g_send.at[d], g_recv.at[d], sibling)

    def gain_out(d):
        sem = CHIPS + d - 1
        return remote(g_fin.at[z, c], g_fin.at[z, c], g_send.at[sem], g_recv.at[sem], at_chip(lax.rem(z + d, CHIPS)))

    def gain_in(d):
        slot, sem = g_fin.at[lax.rem(z + CHIPS - d, CHIPS), c], CHIPS + d - 1
        return remote(slot, slot, g_send.at[sem], g_recv.at[sem], sibling)

    gain_back = remote(g_fin.at[:, c], g_fin.at[:, c], g_send.at[2 * CHIPS - 1], g_recv.at[2 * CHIPS - 1], sibling)
    gain_back_in = remote(g_fin.at[:, o], g_fin.at[:, o], g_send.at[2 * CHIPS - 1], g_recv.at[2 * CHIPS - 1], sibling)

    @pl.loop(0, STEPS)
    def _(s):
        k, i = s // CHUNKS, s % CHUNKS

        @pl.when(s == 2)
        def _():
            load_lp.wait()
            for d in range(1, XS):
                x_wait(d).wait_recv()
            for m in range(YS):
                cols = slice(m * ycols, (m + 1) * ycols)
                ysum[m] = (xr[0, :, cols].astype(F32) + xr[1, :, cols].astype(F32)) + (
                    xr[2, :, cols].astype(F32) + xr[3, :, cols].astype(F32)
                )
            for d in range(1, YS):
                y_copy(d).start()
            yr[y] = ysum[y]

        @pl.when(s == 3)
        def _():
            for d in range(1, YS):
                y_wait(d).wait_recv()
            load_op.wait()
            cols = pl.ds(pl.multiple_of(x * xcols + y * ycols, ycols), ycols)
            total = (yr[0] + yr[1]) + (yr[2] + yr[3])
            zs[...] = (float(XS * YS) * op[:, cols] - total).astype(BF16)

            @pl.when(q == 0)
            def _():
                pl.semaphore_wait(here_sem, 1)

            z_copy.start()

        @pl.when(s == 8)
        def _():
            z_copy.wait_recv()
            ps[x, y] = (zs[...].astype(F32) + zr[...].astype(F32)) * (1.0 / (XS * YS * ZS))
            for d in range(1, YS):
                y_back(d).start()

        @pl.when(s == 9)
        def _():
            for d in range(1, YS):
                y_back_wait(d).wait_recv()
            for d in range(1, XS):
                x_back(d).start()

        @pl.when(s == 10)
        def _():
            for d in range(1, XS):
                x_back_wait(d).wait_recv()
            load_mo.wait()
            rate = OUTER_LR * (step_ref[0].astype(F32) + 1.0) / WARM
            for a in range(XS):
                for b in range(YS):
                    cols = slice((a * YS + b) * ycols, (a * YS + b + 1) * ycols)
                    pseudo = ps[a, b]
                    moment = OUTER_MOMENTUM * mo[:, cols] + pseudo
                    mo[:, cols] = moment
                    op[:, cols] = op[:, cols] - rate * (pseudo + OUTER_MOMENTUM * moment)

        @pl.when(s == LAST)
        def _():
            gain_swap.wait_recv()
            g_own[c] = g_own[c] + g_sib[...]
            for d in range(1, CHIPS):
                gain_copy(d).start()
            g_z[z] = g_own[c, z]

        @pl.when(has_left)
        def _():
            line_copy(s, True).wait_recv()

        @pl.when(has_right)
        def _():
            line_copy(s, False).wait_recv()

        left_weights = jnp.logical_and(has_left, k <= z - 1)
        right_weights = jnp.logical_and(has_right, k <= CHIPS - 2 - z)

        @pl.when(left_weights)
        def _():
            to_sibling(z - 1 - k, i).start()

        @pl.when(right_weights)
        def _():
            to_sibling(z + 1 + k, i).start()

        @pl.when(s == LAST + 1)
        def _():
            for d in range(1, CHIPS):
                gain_wait(d).wait_recv()
            g_fin[z, c] = (g_z[0] + g_z[1]) + (g_z[2] + g_z[3])
            for d in range(1, CHIPS):
                gain_out(d).start()

        @pl.when(s == LAST + 2)
        def _():
            for d in range(1, CHIPS):
                gain_in(d).wait_recv()
            gain_back.start()

        later = k + 1

        @pl.when(jnp.logical_and(has_right, jnp.logical_and(later < CHIPS, later > z)))
        def _():
            add_terms(CHIPS + z - later, i, R0, has_left)

        @pl.when(jnp.logical_and(has_left, jnp.logical_and(later < CHIPS, later > CHIPS - 1 - z)))
        def _():
            add_terms(later + z - CHIPS, i, L0, has_right)

        n = s + CHUNKS - 2 * (s // LAST)
        due = jnp.logical_or(s < LAST - 2, jnp.logical_and(s >= LAST, s < LAST + 2))

        @pl.when(jnp.logical_and(has_right, due))
        def _():
            line_copy(n, True).start()

        @pl.when(jnp.logical_and(has_left, due))
        def _():
            line_copy(n, False).start()

        @pl.when(k == CHIPS - 1)
        def _():
            rows = rows_of(i)
            terms_to_sibling(z, i).wait_recv()
            wg[rows, :] = buf[P0 + 2 * z + c, rows, :].astype(F32) + buf[S0 + z, rows, :].astype(F32)

            @pl.when(has_left)
            def _():
                wg[rows, :] += buf[R0 + z, rows, :].astype(F32)

            @pl.when(has_right)
            def _():
                wg[rows, :] += buf[L0 + z, rows, :].astype(F32)

        @pl.when(left_weights)
        def _():
            use_both(z - 1 - k, i)

        @pl.when(right_weights)
        def _():
            use_both(z + 1 + k, i)

        @pl.when(k == 1)
        def _():
            use_both(z, i)

        @pl.when(s == LAST - 1)
        def _():
            gain_swap.start()
            kout[...] = kacc[...].astype(BF16)

    gain_back_in.wait_recv()

    @pl.when(has_right)
    def _():
        @pl.loop(0, STEPS)
        def _(n):
            line_copy(n, True).wait_send()

    @pl.when(has_left)
    def _():
        @pl.loop(0, STEPS)
        def _(n):
            line_copy(n, False).wait_send()

    @pl.loop(0, STEPS)
    def _(t):
        to_sibling(t // CHUNKS, t % CHUNKS).wait_send()
        terms_to_sibling(t // CHUNKS, t % CHUNKS).wait_send()

    gain_swap.wait_send()
    gain_back.wait_send()
    for d in range(1, CHIPS):
        gain_copy(d).wait_send()
        gain_out(d).wait_send()
    for d in range(1, XS):
        x_copy(d).wait_send()
        x_back(d).wait_send()
    for d in range(1, YS):
        y_copy(d).wait_send()
        y_back(d).wait_send()
    z_copy.wait_send()


def write_out(*refs):
    count = len(refs) // 2
    results, outs, sems = refs[:count], refs[count : 2 * count], refs[-1]
    writes = [pltpu.make_async_copy(a, b, sems.at[i]) for i, (a, b) in enumerate(zip(results, outs))]
    for write in writes:
        write.start()
    for write in writes:
        write.wait()


def local(tokens, key_weight, key_grad, norm_gain, outer_params, local_params, momentum, outer_step):
    rows, width = tokens.shape
    _, shard, kw = key_weight.shape
    frag = outer_params.shape[0]
    xcols, ycols = width // XS, width // XS // YS
    lanes = 128
    dma, anywhere = pltpu.SemaphoreType.DMA, pl.BlockSpec(memory_space=pltpu.HBM)
    results = (
        ((rows, kw), BF16),
        ((shard, kw), F32),
        ((CHIPS, CORES, shard // lanes, lanes), F32),
        (outer_params.shape, F32),
        (momentum.shape, F32),
    )
    held = pl.pallas_call(
        kernel,
        out_shape=tuple(pltpu.VMEM(*result) for result in results),
        in_specs=[anywhere] * 7 + [pl.BlockSpec(memory_space=pltpu.SMEM)],
        out_specs=(pl.BlockSpec(memory_space=pltpu.VMEM),) * 5,
        scratch_shapes=[
            pltpu.VMEM((rows, width), BF16),
            pltpu.VMEM((rows, width), BF16),
            pltpu.VMEM((rows, kw), BF16),
            pltpu.VMEM((1, width), F32),
            pltpu.VMEM((rows, lanes), F32),
            pltpu.VMEM((SLOTS, shard, kw), BF16),
            pltpu.VMEM((rows, kw), F32),
            pltpu.VMEM((CORES, CHIPS, shard // lanes, lanes), F32),
            pltpu.VMEM((CHIPS, shard // lanes, lanes), F32),
            pltpu.VMEM((CHIPS, shard // lanes, lanes), F32),
            pltpu.VMEM((XS, frag, xcols), BF16),
            pltpu.VMEM((YS, frag, ycols), F32),
            pltpu.VMEM((YS, frag, ycols), F32),
            pltpu.VMEM((frag, ycols), BF16),
            pltpu.VMEM((frag, ycols), BF16),
            pltpu.VMEM((XS, YS, frag, ycols), F32),
            dma((LOADS,)),
            dma((6,)),
            dma((STEPS,)),
            dma((STEPS,)),
            dma((STEPS,)),
            dma((STEPS,)),
            dma((CHIPS, CHUNKS)),
            dma((CHIPS, CHUNKS)),
            dma((CHIPS, CHUNKS)),
            dma((CHIPS, CHUNKS)),
            dma((2 * CHIPS,)),
            dma((2 * CHIPS,)),
            dma((5, 3)),
            dma((5, 3)),
            pltpu.SemaphoreType.REGULAR,
        ],
        compiler_params=pltpu.CompilerParams(
            collective_id=0, has_side_effects=True, vmem_limit_bytes=54 * MIB
        ),
        cost_estimate=pl.CostEstimate(
            flops=6 * rows * width * kw, bytes_accessed=16 * MIB, transcendentals=rows
        ),
        name="outer_and_keys",
    )(
        tokens, key_weight[0], key_grad, norm_gain, outer_params, local_params[0], momentum, outer_step
    )
    keys, weight_grad, gain_grad, new_outer, new_momentum = pl.pallas_call(
        write_out,
        out_shape=tuple(jax.ShapeDtypeStruct(*result) for result in results),
        in_specs=[pl.BlockSpec(memory_space=pltpu.VMEM)] * len(results),
        out_specs=(anywhere,) * len(results),
        scratch_shapes=[dma((len(results),))],
        compiler_params=pltpu.CompilerParams(vmem_limit_bytes=MIB),
        name="write_out",
    )(*[pltpu.with_memory_space_constraint(a, pltpu.VMEM) for a in held])
    return keys, weight_grad[None], gain_grad.reshape(1, width), new_outer, new_momentum


def solution(mesh):
    placed = (
        P(("rep", "fsdp"), None),
        P("rep", "fsdp", None),
        P(("rep", "fsdp"), None),
        P("rep", None),
        P("fsdp", None),
        P("rep", "fsdp", None),
        P("fsdp", None),
        P(),
    )
    return jax.shard_map(
        local,
        mesh=mesh,
        in_specs=placed,
        out_specs=(
            P(("rep", "fsdp"), None),
            P("rep", "fsdp", None),
            P("rep", None),
            P("fsdp", None),
            P("fsdp", None),
        ),
        check_vma=False,
    )
```

```python
import functools

import jax
import jax.numpy as jnp
from jax import lax
from jax.experimental import pallas as pl
from jax.experimental.pallas import tpu as pltpu
from jax.sharding import PartitionSpec as P

MESH = pl.DeviceIdType.MESH
BF16, F32 = jnp.bfloat16, jnp.float32

WARM = 8
EPSILON = 1e-05
OUTER_LR = 0.7
OUTER_MOMENTUM = 0.9

CHIPS, CORES = 4, 2
XS, YS, ZS = 4, 4, 2
CHUNKS = 4
STEPS = CHIPS * CHUNKS
LAST = STEPS - CHUNKS
LOADS = 6
ROWS = 16
PIECES = (1, 1, 1, 1, 1)
MIB = 1024 * 1024

W0, P0, S0, R0, L0 = 0, 8, 16, 20, 24
SLOTS = 28


def kernel(
    tok_hbm, kw_hbm, kg_hbm, gain_hbm, op_hbm, lp_hbm, mo_hbm, step_hbm,
    kout, wg, g_fin, op, mo,
    tok, nrm, kg, gain, inv, buf, kacc,
    g_own, g_sib, g_z,
    xr, ysum, yr, zs, zr, ps,
    step_ref, tok_sem, ld_sem,
    r_send, r_recv, l_send, l_recv,
    w_send, w_recv, p_send, p_recv,
    g_send, g_recv, o_send, o_recv, here_sem, line_sem, all_sem,
):
    tokens, width = tok.shape
    shard, kw = buf.shape[1:]
    part = shard // CHUNKS
    frag = op.shape[0]
    xcols, ycols = width // XS, width // XS // YS

    rep, fsdp = lax.axis_index("rep"), lax.axis_index("fsdp")
    q, x, y = rep // (XS * YS), (rep // YS) % XS, rep % YS
    z, c = fsdp // CORES, fsdp % CORES
    o = 1 - c

    def at_rep(q_, x_, y_):
        return ((q_ * XS + x_) * YS + y_, fsdp)

    def at_chip(z_):
        return (rep, z_ * CORES + c)

    sibling = (rep, z * CORES + o)
    right, left = at_chip(lax.rem(z + 1, CHIPS)), at_chip(lax.rem(z + CHIPS - 1, CHIPS))
    has_right, has_left = z < CHIPS - 1, z > 0

    def remote(src, dst, send, recv, device):
        return pltpu.make_async_remote_copy(
            src_ref=src, dst_ref=dst, send_sem=send, recv_sem=recv, device_id=device, device_id_type=MESH
        )

    def rows_of(i):
        return pl.ds(pl.multiple_of(i * part, part), part)

    barrier = pltpu.get_barrier_semaphore()
    partner = at_rep(1 - q, x, y)

    def greet(peer):
        pl.semaphore_signal(barrier, inc=1, device_id=peer, device_id_type=MESH)

    def answer(peer):
        pl.semaphore_signal(here_sem, inc=1, device_id=peer, device_id_type=MESH)

    def wait_for(sem, count):
        @pl.when(count > 0)
        def _():
            pl.semaphore_wait(sem, count)

    both = jnp.logical_and(has_right, q == 1)

    @pl.when(has_right)
    def _():
        greet(right)

    @pl.when(jnp.logical_and(has_left, q == 1))
    def _():
        greet(left)

    @pl.when(c == 1)
    def _():
        greet(sibling)

    @pl.when(x == 0)
    def _():
        for d in range(1, XS):
            greet(at_rep(q, d, y))

    @pl.when(y == 0)
    def _():
        for d in range(1, YS):
            greet(at_rep(q, x, d))

    @pl.when(q == 0)
    def _():
        greet(partner)

    x_later, y_later = (x > 0).astype(jnp.int32), (y > 0).astype(jnp.int32)
    wait_for(barrier, has_left.astype(jnp.int32) + both.astype(jnp.int32) + o + x_later + y_later + q)

    @pl.when(jnp.logical_and(has_left, q == 0))
    def _():
        pl.semaphore_signal(line_sem, inc=1, device_id=left, device_id_type=MESH)

    block = tokens // LOADS

    def tok_load(b):
        rows = pl.ds(pl.multiple_of(b * block, block), block)
        return pltpu.make_async_copy(tok_hbm.at[rows], tok.at[rows], tok_sem.at[b])

    load_gain = pltpu.make_async_copy(gain_hbm, gain, ld_sem.at[0])
    load_kg = pltpu.make_async_copy(kg_hbm, kg, ld_sem.at[1])
    load_w = pltpu.make_async_copy(kw_hbm, buf.at[W0 + 2 * z + c], ld_sem.at[2])
    own_x = pl.ds(pl.multiple_of(x * xcols, xcols), xcols)
    load_lp = pltpu.make_async_copy(lp_hbm.at[:, own_x], xr.at[x], ld_sem.at[3])
    load_op = pltpu.make_async_copy(op_hbm, op, ld_sem.at[4])
    load_mo = pltpu.make_async_copy(mo_hbm, mo, ld_sem.at[5])
    load_step = pltpu.make_async_copy(step_hbm, step_ref, ld_sem.at[6])

    def line_first(n, rightward):
        rows = rows_of(n)
        dst = buf.at[W0 + 2 * z + c, rows]
        if rightward:
            return remote(kw_hbm.at[rows], dst, r_send.at[n], r_recv.at[n], right)
        return remote(kw_hbm.at[rows], dst, l_send.at[n], l_recv.at[n], left)

    def line_copy(n, rightward):
        k, rows = n // CHUNKS, rows_of(n % CHUNKS)
        if rightward:
            is_sum = (k - z + CHIPS - 1) // CHIPS
            weight, owner = 2 * (z - k) + c, CHIPS + z - k
            src = (1 - is_sum) * (W0 + weight) + is_sum * (P0 + 2 * owner + c)
            dst = (1 - is_sum) * (W0 + weight) + is_sum * (R0 + owner)
            return remote(buf.at[src, rows], buf.at[dst, rows], r_send.at[n], r_recv.at[n], right)
        is_sum = (k + z) // CHIPS
        weight, owner = 2 * (z + k) + c, k + z - CHIPS
        src = (1 - is_sum) * (W0 + weight) + is_sum * (P0 + 2 * owner + c)
        dst = (1 - is_sum) * (W0 + weight) + is_sum * (L0 + owner)
        return remote(buf.at[src, rows], buf.at[dst, rows], l_send.at[n], l_recv.at[n], left)

    @pl.when(has_left)
    def _():
        for n in range(CHUNKS):
            line_first(n, False).start()

    @pl.when(jnp.logical_and(has_right, q == 0))
    def _():
        pl.semaphore_wait(line_sem, 1)

    @pl.when(has_right)
    def _():
        for n in range(CHUNKS):
            line_first(n, True).start()

    load_gain.start()
    tok_load(0).start()
    load_kg.start()
    for b in range(1, LOADS):
        tok_load(b).start()
    for load in (load_w, load_lp, load_op, load_mo, load_step):
        load.start()

    def own_to_sibling(i):
        rows = rows_of(i)
        return remote(
            kw_hbm.at[rows], buf.at[W0 + 2 * z + c, rows], w_send.at[z, i], w_recv.at[z, i], sibling
        )

    def to_sibling(a, i):
        there = buf.at[W0 + 2 * a + c, rows_of(i)]
        return remote(there, there, w_send.at[a, i], w_recv.at[a, i], sibling)

    def from_sibling(a, i):
        there = buf.at[W0 + 2 * a + o, rows_of(i)]
        return remote(there, there, w_send.at[a, i], w_recv.at[a, i], sibling)

    def terms_to_sibling(j, i):
        return remote(
            buf.at[P0 + 2 * j + o, rows_of(i)], buf.at[S0 + j, rows_of(i)], p_send.at[j, i], p_recv.at[j, i], sibling
        )

    def x_copy(d):
        to = lax.rem(x + d, XS)
        cols = pl.ds(pl.multiple_of(to * xcols, xcols), xcols)
        return remote(lp_hbm.at[:, cols], xr.at[x], o_send.at[0, d - 1], o_recv.at[0, d - 1], at_rep(q, to, y))

    def x_wait(d):
        slot = xr.at[lax.rem(x + XS - d, XS)]
        return remote(slot, slot, o_send.at[0, d - 1], o_recv.at[0, d - 1], sibling)

    def y_copy(d):
        to = lax.rem(y + d, YS)
        return remote(ysum.at[to], yr.at[y], o_send.at[1, d - 1], o_recv.at[1, d - 1], at_rep(q, x, to))

    def y_wait(d):
        slot = yr.at[lax.rem(y + YS - d, YS)]
        return remote(slot, slot, o_send.at[1, d - 1], o_recv.at[1, d - 1], sibling)

    z_copy = remote(zs, zr, o_send.at[2, 0], o_recv.at[2, 0], partner)

    def y_back(d):
        piece = ps.at[x, y]
        return remote(
            piece, piece, o_send.at[3, d - 1], o_recv.at[3, d - 1], at_rep(q, x, lax.rem(y + d, YS))
        )

    def y_back_wait(d):
        piece = ps.at[x, lax.rem(y + YS - d, YS)]
        return remote(piece, piece, o_send.at[3, d - 1], o_recv.at[3, d - 1], sibling)

    def x_back(d):
        piece = ps.at[x]
        return remote(
            piece, piece, o_send.at[4, d - 1], o_recv.at[4, d - 1], at_rep(q, lax.rem(x + d, XS), y)
        )

    def x_back_wait(d):
        piece = ps.at[lax.rem(x + XS - d, XS)]
        return remote(piece, piece, o_send.at[4, d - 1], o_recv.at[4, d - 1], sibling)

    @pl.when(x > 0)
    def _():
        answer(at_rep(q, 0, y))

    @pl.when(y > 0)
    def _():
        answer(at_rep(q, x, 0))

    @pl.when(q == 1)
    def _():
        answer(partner)

    @pl.when(c == 0)
    def _():
        answer(sibling)

    load_gain.wait()
    lanes = 128
    pieces = width // lanes

    @pl.loop(0, LOADS)
    def _(b):
        tok_load(b).wait()

        @pl.loop(0, block // ROWS)
        def _(r):
            rows = pl.ds(pl.multiple_of(b * block + r * ROWS, ROWS), ROWS)
            sums = [jnp.zeros((ROWS, lanes), F32) for _ in range(4)]
            for m in range(pieces):
                wide = tok[rows, m * lanes : (m + 1) * lanes].astype(F32)
                sums[m % 4] = sums[m % 4] + wide * wide
            total = jnp.sum((sums[0] + sums[1]) + (sums[2] + sums[3]), axis=1, keepdims=True)
            scale = jnp.broadcast_to(lax.rsqrt(total * (1.0 / width) + EPSILON), (ROWS, lanes))
            inv[rows, :] = scale
            for m in range(pieces):
                cols = slice(m * lanes, (m + 1) * lanes)
                nrm[rows, cols] = (tok[rows, cols].astype(F32) * scale * gain[:, cols]).astype(BF16)

    wait_for(here_sem, (1 - x_later) * (XS - 1) + (1 - y_later) * (YS - 1) + (ZS - 1 - q) + c)

    @pl.when(x == 0)
    def _():
        for d in range(1, XS):
            pl.semaphore_signal(all_sem, inc=1, device_id=at_rep(q, d, y), device_id_type=MESH)

    @pl.when(y == 0)
    def _():
        for d in range(1, YS):
            pl.semaphore_signal(all_sem, inc=1, device_id=at_rep(q, x, d), device_id_type=MESH)

    for i in range(CHUNKS):
        own_to_sibling(i).start()

    load_kg.wait()
    upper = z // (CHIPS // 2)

    def cols_of(owner, i):
        return pl.ds(pl.multiple_of(owner * shard + i * part, part), part)

    def terms(owner, i):
        got = lax.dot_general(
            nrm[:, cols_of(owner, i)], kg[...], (((0,), (0,)), ((), ())), preferred_element_type=F32
        )
        buf[P0 + owner, rows_of(i), :] = got.astype(BF16)

    @pl.loop(0, STEPS)
    def _(t):
        n, i = t // CHUNKS, t % CHUNKS
        j = (1 - upper) * (CHIPS - 1 - n) + upper * n
        terms(2 * j + o, i)
        terms_to_sibling(j, i).start()
        terms(2 * j + c, i)

    wait_for(all_sem, x_later + y_later)
    for d in range(1, XS):
        x_copy(d).start()

    kacc[...] = jnp.zeros_like(kacc)
    load_w.wait()

    def use_rows(a, core, i):
        owner = 2 * a + core
        rows = buf[W0 + owner, rows_of(i), :]
        cols = cols_of(owner, i)
        kacc[...] += jnp.dot(nrm[:, cols], rows, preferred_element_type=F32)
        d_normed = lax.dot_general(kg[...], rows, (((1,), (1,)), ((), ())), preferred_element_type=F32)
        wide = tok[:, cols].astype(F32)
        for m in range(part // lanes):
            here = slice(m * lanes, (m + 1) * lanes)
            got = jnp.sum(d_normed[:, here] * wide[:, here] * inv[...], axis=0, keepdims=True)
            g_own[core, a, pl.ds(i * (part // lanes) + m, 1), :] = got

    def use_both(a, i):
        use_rows(a, c, i)
        from_sibling(a, i).wait_recv()
        use_rows(a, o, i)

    def add_terms(j, i, base, from_line):
        rows = rows_of(i)
        terms_to_sibling(j, i).wait_recv()
        own = buf[P0 + 2 * j + c, rows, :].astype(F32) + buf[S0 + j, rows, :].astype(F32)

        @pl.when(from_line)
        def _():
            buf[P0 + 2 * j + c, rows, :] = (own + buf[base + j, rows, :].astype(F32)).astype(BF16)

        @pl.when(jnp.logical_not(from_line))
        def _():
            buf[P0 + 2 * j + c, rows, :] = own.astype(BF16)

    gain_swap = remote(g_own.at[o], g_sib, g_send.at[0], g_recv.at[0], sibling)

    def gain_copy(d):
        to = lax.rem(z + d, CHIPS)
        return remote(g_own.at[c, to], g_z.at[z], g_send.at[d], g_recv.at[d], at_chip(to))

    def gain_wait(d):
        slot = g_z.at[lax.rem(z + CHIPS - d, CHIPS)]
        return remote(slot, slot, g_send.at[d], g_recv.at[d], sibling)

    def gain_out(d):
        sem = CHIPS + d - 1
        return remote(g_fin.at[z, c], g_fin.at[z, c], g_send.at[sem], g_recv.at[sem], at_chip(lax.rem(z + d, CHIPS)))

    def gain_in(d):
        slot, sem = g_fin.at[lax.rem(z + CHIPS - d, CHIPS), c], CHIPS + d - 1
        return remote(slot, slot, g_send.at[sem], g_recv.at[sem], sibling)

    gain_back = remote(g_fin.at[:, c], g_fin.at[:, c], g_send.at[2 * CHIPS - 1], g_recv.at[2 * CHIPS - 1], sibling)
    gain_back_in = remote(g_fin.at[:, o], g_fin.at[:, o], g_send.at[2 * CHIPS - 1], g_recv.at[2 * CHIPS - 1], sibling)

    @pl.loop(0, STEPS)
    def _(s):
        k, i = s // CHUNKS, s % CHUNKS

        @pl.when(s == 2)
        def _():
            load_lp.wait()
            for d in range(1, XS):
                x_wait(d).wait_recv()
            for m in range(YS):
                cols = slice(m * ycols, (m + 1) * ycols)
                ysum[m] = (xr[0, :, cols].astype(F32) + xr[1, :, cols].astype(F32)) + (
                    xr[2, :, cols].astype(F32) + xr[3, :, cols].astype(F32)
                )
            for d in range(1, YS):
                y_copy(d).start()
            yr[y] = ysum[y]

        @pl.when(s == 4)
        def _():
            for d in range(1, YS):
                y_wait(d).wait_recv()
            load_op.wait()
            cols = pl.ds(pl.multiple_of(x * xcols + y * ycols, ycols), ycols)
            total = (yr[0] + yr[1]) + (yr[2] + yr[3])
            zs[...] = (float(XS * YS) * op[:, cols] - total).astype(BF16)
            z_copy.start()

        @pl.when(s == 9)
        def _():
            z_copy.wait_recv()
            ps[x, y] = (zs[...].astype(F32) + zr[...].astype(F32)) * (1.0 / (XS * YS * ZS))
            for d in range(1, YS):
                y_back(d).start()

        @pl.when(s == 10)
        def _():
            for d in range(1, YS):
                y_back_wait(d).wait_recv()
            for d in range(1, XS):
                x_back(d).start()

        @pl.when(s == STEPS - 2)
        def _():
            for d in range(1, XS):
                x_back_wait(d).wait_recv()
            load_mo.wait()
            load_step.wait()
            rate = OUTER_LR * (step_ref[0].astype(F32) + 1.0) / WARM
            for a in range(XS):
                for b in range(YS):
                    cols = slice((a * YS + b) * ycols, (a * YS + b + 1) * ycols)
                    pseudo = ps[a, b]
                    moment = OUTER_MOMENTUM * mo[:, cols] + pseudo
                    mo[:, cols] = moment
                    op[:, cols] = op[:, cols] - rate * (pseudo + OUTER_MOMENTUM * moment)

        @pl.when(s == LAST + 1)
        def _():
            for d in range(1, CHIPS):
                gain_wait(d).wait_recv()
            g_fin[z, c] = (g_z[0] + g_z[1]) + (g_z[2] + g_z[3])
            for d in range(1, CHIPS):
                gain_out(d).start()

        @pl.when(s == STEPS - 1)
        def _():
            for d in range(1, CHIPS):
                gain_in(d).wait_recv()
            gain_back.start()

        @pl.when(jnp.logical_and(has_right, s > 1))
        def _():
            line_copy(s - 2, True).wait_send()

        @pl.when(jnp.logical_and(has_left, s > 1))
        def _():
            line_copy(s - 2, False).wait_send()

        @pl.when(k == CHIPS - 1)
        def _():
            for a in range(CHIPS):
                to_sibling(a, i).wait_send()
                terms_to_sibling(a, i).wait_send()

        @pl.when(s == LAST + 1)
        def _():
            gain_swap.wait_send()
            for d in range(1, XS):
                x_copy(d).wait_send()
                x_back(d).wait_send()
            for d in range(1, YS):
                y_copy(d).wait_send()
                y_back(d).wait_send()
            z_copy.wait_send()

        @pl.when(s == STEPS - 1)
        def _():
            for d in range(1, CHIPS):
                gain_copy(d).wait_send()
                gain_out(d).wait_send()

        @pl.when(k == CHIPS - 1)
        def _():
            rows = rows_of(i)
            terms_to_sibling(z, i).wait_recv()
            wg[rows, :] = buf[P0 + 2 * z + c, rows, :].astype(F32) + buf[S0 + z, rows, :].astype(F32)

        @pl.when(has_left)
        def _():
            line_copy(s, True).wait_recv()

        @pl.when(has_right)
        def _():
            line_copy(s, False).wait_recv()

        left_weights = jnp.logical_and(has_left, k <= z - 1)
        right_weights = jnp.logical_and(has_right, k <= CHIPS - 2 - z)

        @pl.when(left_weights)
        def _():
            to_sibling(z - 1 - k, i).start()

        @pl.when(right_weights)
        def _():
            to_sibling(z + 1 + k, i).start()

        @pl.when(left_weights)
        def _():
            use_both(z - 1 - k, i)

        @pl.when(right_weights)
        def _():
            use_both(z + 1 + k, i)

        @pl.when(k == 1)
        def _():
            use_both(z, i)

        @pl.when(s == LAST - 1)
        def _():
            gain_swap.start()
            kout[...] = kacc[...].astype(BF16)

        later = k + 1

        @pl.when(jnp.logical_and(has_right, jnp.logical_and(later < CHIPS, later > z)))
        def _():
            add_terms(CHIPS + z - later, i, R0, has_left)

        @pl.when(jnp.logical_and(has_left, jnp.logical_and(later < CHIPS, later > CHIPS - 1 - z)))
        def _():
            add_terms(later + z - CHIPS, i, L0, has_right)

        @pl.when(s == LAST - 1)
        def _():
            gain_swap.wait_recv()
            g_own[c] = g_own[c] + g_sib[...]
            for d in range(1, CHIPS):
                gain_copy(d).start()
            g_z[z] = g_own[c, z]

        early, late = s < LAST + 1 - CHUNKS, jnp.logical_and(s >= LAST - 1, s < LAST + 2)
        n = s + CHUNKS - (CHUNKS - 2) * late.astype(jnp.int32)
        due = jnp.logical_or(early, late)

        @pl.when(jnp.logical_and(has_right, due))
        def _():
            line_copy(n, True).start()

        @pl.when(jnp.logical_and(has_left, due))
        def _():
            line_copy(n, False).start()

        @pl.when(jnp.logical_and(has_left, k == CHIPS - 1))
        def _():
            wg[rows_of(i), :] += buf[R0 + z, rows_of(i), :].astype(F32)

        @pl.when(jnp.logical_and(has_right, k == CHIPS - 1))
        def _():
            wg[rows_of(i), :] += buf[L0 + z, rows_of(i), :].astype(F32)

    gain_back_in.wait_recv()
    gain_back.wait_send()

    @pl.when(has_right)
    def _():
        line_copy(STEPS - 2, True).wait_send()
        line_copy(STEPS - 1, True).wait_send()

    @pl.when(has_left)
    def _():
        line_copy(STEPS - 2, False).wait_send()
        line_copy(STEPS - 1, False).wait_send()


def write_out(*refs):
    count = len(PIECES)
    results, outs, sems = refs[:count], refs[count : 2 * count], refs[-1]
    writes = []
    for result, out, pieces in zip(results, outs, PIECES):
        size = result.shape[0] // pieces
        for i in range(pieces):
            here = pl.ds(i * size, size)
            writes.append(pltpu.make_async_copy(result.at[here], out.at[here], sems.at[len(writes)]))
    for write in writes:
        write.start()
    for write in writes:
        write.wait()


def local(tokens, key_weight, key_grad, norm_gain, outer_params, local_params, momentum, outer_step):
    rows, width = tokens.shape
    _, shard, kw = key_weight.shape
    frag = outer_params.shape[0]
    xcols, ycols = width // XS, width // XS // YS
    lanes = 128
    dma, anywhere = pltpu.SemaphoreType.DMA, pl.BlockSpec(memory_space=pltpu.HBM)
    results = (
        ((rows, kw), BF16),
        ((shard, kw), F32),
        ((CHIPS, CORES, shard // lanes, lanes), F32),
        (outer_params.shape, F32),
        (momentum.shape, F32),
    )
    held = pl.pallas_call(
        kernel,
        out_shape=tuple(pltpu.VMEM(*result) for result in results),
        in_specs=[anywhere] * 8,
        out_specs=(pl.BlockSpec(memory_space=pltpu.VMEM),) * 5,
        scratch_shapes=[
            pltpu.VMEM((rows, width), BF16),
            pltpu.VMEM((rows, width), BF16),
            pltpu.VMEM((rows, kw), BF16),
            pltpu.VMEM((1, width), F32),
            pltpu.VMEM((rows, lanes), F32),
            pltpu.VMEM((SLOTS, shard, kw), BF16),
            pltpu.VMEM((rows, kw), F32),
            pltpu.VMEM((CORES, CHIPS, shard // lanes, lanes), F32),
            pltpu.VMEM((CHIPS, shard // lanes, lanes), F32),
            pltpu.VMEM((CHIPS, shard // lanes, lanes), F32),
            pltpu.VMEM((XS, frag, xcols), BF16),
            pltpu.VMEM((YS, frag, ycols), F32),
            pltpu.VMEM((YS, frag, ycols), F32),
            pltpu.VMEM((frag, ycols), BF16),
            pltpu.VMEM((frag, ycols), BF16),
            pltpu.VMEM((XS, YS, frag, ycols), F32),
            pltpu.SMEM((1,), jnp.int32),
            dma((LOADS,)),
            dma((7,)),
            dma((STEPS,)),
            dma((STEPS,)),
            dma((STEPS,)),
            dma((STEPS,)),
            dma((CHIPS, CHUNKS)),
            dma((CHIPS, CHUNKS)),
            dma((CHIPS, CHUNKS)),
            dma((CHIPS, CHUNKS)),
            dma((2 * CHIPS,)),
            dma((2 * CHIPS,)),
            dma((5, 3)),
            dma((5, 3)),
            pltpu.SemaphoreType.REGULAR,
            pltpu.SemaphoreType.REGULAR,
            pltpu.SemaphoreType.REGULAR,
        ],
        compiler_params=pltpu.CompilerParams(
            collective_id=0, has_side_effects=True, vmem_limit_bytes=54 * MIB
        ),
        cost_estimate=pl.CostEstimate(
            flops=6 * rows * width * kw, bytes_accessed=16 * MIB, transcendentals=rows
        ),
        name="outer_and_keys",
    )(
        tokens, key_weight[0], key_grad, norm_gain, outer_params, local_params[0], momentum, outer_step
    )
    keys, weight_grad, gain_grad, new_outer, new_momentum = pl.pallas_call(
        write_out,
        out_shape=tuple(jax.ShapeDtypeStruct(*result) for result in results),
        in_specs=[pl.BlockSpec(memory_space=pltpu.VMEM)] * len(results),
        out_specs=(anywhere,) * len(results),
        scratch_shapes=[dma((sum(PIECES),))],
        compiler_params=pltpu.CompilerParams(vmem_limit_bytes=MIB),
        name="write_out",
    )(*[pltpu.with_memory_space_constraint(a, pltpu.VMEM) for a in held])
    return keys, weight_grad[None], gain_grad.reshape(1, width), new_outer, new_momentum


def solution(mesh):
    placed = (
        P(("rep", "fsdp"), None),
        P("rep", "fsdp", None),
        P(("rep", "fsdp"), None),
        P("rep", None),
        P("fsdp", None),
        P("rep", "fsdp", None),
        P("fsdp", None),
        P(),
    )
    return jax.shard_map(
        local,
        mesh=mesh,
        in_specs=placed,
        out_specs=(
            P(("rep", "fsdp"), None),
            P("rep", "fsdp", None),
            P("rep", None),
            P("fsdp", None),
            P("fsdp", None),
        ),
        check_vma=False,
    )
```

```python
import functools

import jax
import jax.numpy as jnp
from jax import lax
from jax.experimental import pallas as pl
from jax.experimental.pallas import tpu as pltpu
from jax.sharding import PartitionSpec as P

MESH = pl.DeviceIdType.MESH
BF16, F32 = jnp.bfloat16, jnp.float32

WARM = 8
EPSILON = 1e-05
OUTER_LR = 0.7
OUTER_MOMENTUM = 0.9

CHIPS, CORES = 4, 2
XS, YS, ZS = 4, 4, 2
CHUNKS = 4
STEPS = CHIPS * CHUNKS
LAST = STEPS - CHUNKS
LOADS = 6
ROWS = 16
PIECES = (1, 1, 1, 1, 1)
MIB = 1024 * 1024

W0, P0, S0, R0, L0 = 0, 8, 16, 20, 24
SLOTS = 28


def kernel(
    tok_hbm, kw_hbm, kg_hbm, gain_hbm, op_hbm, lp_hbm, mo_hbm, step_hbm,
    kout, wg, g_fin, op, mo,
    tok, nrm, kg, gain, inv, buf, kacc,
    g_own, g_sib, g_z,
    xr, ysum, yr, zs, zr, ps,
    step_ref, tok_sem, ld_sem,
    r_send, r_recv, l_send, l_recv,
    w_send, w_recv, p_send, p_recv,
    g_send, g_recv, o_send, o_recv, here_sem, line_sem, all_sem,
):
    tokens, width = tok.shape
    shard, kw = buf.shape[1:]
    part = shard // CHUNKS
    frag = op.shape[0]
    xcols, ycols = width // XS, width // XS // YS

    rep, fsdp = lax.axis_index("rep"), lax.axis_index("fsdp")
    q, x, y = rep // (XS * YS), (rep // YS) % XS, rep % YS
    z, c = fsdp // CORES, fsdp % CORES
    o = 1 - c

    def at_rep(q_, x_, y_):
        return ((q_ * XS + x_) * YS + y_, fsdp)

    def at_chip(z_):
        return (rep, z_ * CORES + c)

    sibling = (rep, z * CORES + o)
    right, left = at_chip(lax.rem(z + 1, CHIPS)), at_chip(lax.rem(z + CHIPS - 1, CHIPS))
    has_right, has_left = z < CHIPS - 1, z > 0

    def remote(src, dst, send, recv, device):
        return pltpu.make_async_remote_copy(
            src_ref=src, dst_ref=dst, send_sem=send, recv_sem=recv, device_id=device, device_id_type=MESH
        )

    def rows_of(i):
        return pl.ds(pl.multiple_of(i * part, part), part)

    barrier = pltpu.get_barrier_semaphore()
    partner = at_rep(1 - q, x, y)

    def greet(peer):
        pl.semaphore_signal(barrier, inc=1, device_id=peer, device_id_type=MESH)

    def answer(peer):
        pl.semaphore_signal(here_sem, inc=1, device_id=peer, device_id_type=MESH)

    def wait_for(sem, count):
        @pl.when(count > 0)
        def _():
            pl.semaphore_wait(sem, count)

    both = jnp.logical_and(has_right, q == 1)

    @pl.when(has_right)
    def _():
        greet(right)

    @pl.when(jnp.logical_and(has_left, q == 1))
    def _():
        greet(left)

    @pl.when(c == 1)
    def _():
        greet(sibling)

    @pl.when(x == 0)
    def _():
        for d in range(1, XS):
            greet(at_rep(q, d, y))

    @pl.when(y == 0)
    def _():
        for d in range(1, YS):
            greet(at_rep(q, x, d))

    @pl.when(q == 0)
    def _():
        greet(partner)

    x_later, y_later = (x > 0).astype(jnp.int32), (y > 0).astype(jnp.int32)
    wait_for(barrier, has_left.astype(jnp.int32) + both.astype(jnp.int32) + o + x_later + y_later + q)

    @pl.when(jnp.logical_and(has_left, q == 0))
    def _():
        pl.semaphore_signal(line_sem, inc=1, device_id=left, device_id_type=MESH)

    block = tokens // LOADS

    def tok_load(b):
        rows = pl.ds(pl.multiple_of(b * block, block), block)
        return pltpu.make_async_copy(tok_hbm.at[rows], tok.at[rows], tok_sem.at[b])

    load_gain = pltpu.make_async_copy(gain_hbm, gain, ld_sem.at[0])
    load_kg = pltpu.make_async_copy(kg_hbm, kg, ld_sem.at[1])
    load_w = pltpu.make_async_copy(kw_hbm, buf.at[W0 + 2 * z + c], ld_sem.at[2])
    own_x = pl.ds(pl.multiple_of(x * xcols, xcols), xcols)
    load_lp = pltpu.make_async_copy(lp_hbm.at[:, own_x], xr.at[x], ld_sem.at[3])
    load_op = pltpu.make_async_copy(op_hbm, op, ld_sem.at[4])
    load_mo = pltpu.make_async_copy(mo_hbm, mo, ld_sem.at[5])
    load_step = pltpu.make_async_copy(step_hbm, step_ref, ld_sem.at[6])

    def line_first(n, rightward):
        rows = rows_of(n)
        dst = buf.at[W0 + 2 * z + c, rows]
        if rightward:
            return remote(kw_hbm.at[rows], dst, r_send.at[n], r_recv.at[n], right)
        return remote(kw_hbm.at[rows], dst, l_send.at[n], l_recv.at[n], left)

    def line_copy(n, rightward):
        k, rows = n // CHUNKS, rows_of(n % CHUNKS)
        if rightward:
            is_sum = (k - z + CHIPS - 1) // CHIPS
            weight, owner = 2 * (z - k) + c, CHIPS + z - k
            src = (1 - is_sum) * (W0 + weight) + is_sum * (P0 + 2 * owner + c)
            dst = (1 - is_sum) * (W0 + weight) + is_sum * (R0 + owner)
            return remote(buf.at[src, rows], buf.at[dst, rows], r_send.at[n], r_recv.at[n], right)
        is_sum = (k + z) // CHIPS
        weight, owner = 2 * (z + k) + c, k + z - CHIPS
        src = (1 - is_sum) * (W0 + weight) + is_sum * (P0 + 2 * owner + c)
        dst = (1 - is_sum) * (W0 + weight) + is_sum * (L0 + owner)
        return remote(buf.at[src, rows], buf.at[dst, rows], l_send.at[n], l_recv.at[n], left)

    @pl.when(has_left)
    def _():
        for n in range(CHUNKS):
            line_first(n, False).start()

    @pl.when(jnp.logical_and(has_right, q == 0))
    def _():
        pl.semaphore_wait(line_sem, 1)

    @pl.when(has_right)
    def _():
        for n in range(CHUNKS):
            line_first(n, True).start()

    load_gain.start()
    tok_load(0).start()
    load_kg.start()
    for b in range(1, LOADS):
        tok_load(b).start()
    for load in (load_w, load_lp, load_op, load_mo, load_step):
        load.start()

    def own_to_sibling(i):
        rows = rows_of(i)
        return remote(
            kw_hbm.at[rows], buf.at[W0 + 2 * z + c, rows], w_send.at[z, i], w_recv.at[z, i], sibling
        )

    def to_sibling(a, i):
        there = buf.at[W0 + 2 * a + c, rows_of(i)]
        return remote(there, there, w_send.at[a, i], w_recv.at[a, i], sibling)

    def from_sibling(a, i):
        there = buf.at[W0 + 2 * a + o, rows_of(i)]
        return remote(there, there, w_send.at[a, i], w_recv.at[a, i], sibling)

    def terms_to_sibling(j, i):
        return remote(
            buf.at[P0 + 2 * j + o, rows_of(i)], buf.at[S0 + j, rows_of(i)], p_send.at[j, i], p_recv.at[j, i], sibling
        )

    def x_copy(d):
        to = lax.rem(x + d, XS)
        cols = pl.ds(pl.multiple_of(to * xcols, xcols), xcols)
        return remote(lp_hbm.at[:, cols], xr.at[x], o_send.at[0, d - 1], o_recv.at[0, d - 1], at_rep(q, to, y))

    def x_wait(d):
        slot = xr.at[lax.rem(x + XS - d, XS)]
        return remote(slot, slot, o_send.at[0, d - 1], o_recv.at[0, d - 1], sibling)

    def y_copy(d):
        to = lax.rem(y + d, YS)
        return remote(ysum.at[to], yr.at[y], o_send.at[1, d - 1], o_recv.at[1, d - 1], at_rep(q, x, to))

    def y_wait(d):
        slot = yr.at[lax.rem(y + YS - d, YS)]
        return remote(slot, slot, o_send.at[1, d - 1], o_recv.at[1, d - 1], sibling)

    z_copy = remote(zs, zr, o_send.at[2, 0], o_recv.at[2, 0], partner)

    def y_back(d):
        piece = ps.at[x, y]
        return remote(
            piece, piece, o_send.at[3, d - 1], o_recv.at[3, d - 1], at_rep(q, x, lax.rem(y + d, YS))
        )

    def y_back_wait(d):
        piece = ps.at[x, lax.rem(y + YS - d, YS)]
        return remote(piece, piece, o_send.at[3, d - 1], o_recv.at[3, d - 1], sibling)

    def x_back(d):
        piece = ps.at[x]
        return remote(
            piece, piece, o_send.at[4, d - 1], o_recv.at[4, d - 1], at_rep(q, lax.rem(x + d, XS), y)
        )

    def x_back_wait(d):
        piece = ps.at[lax.rem(x + XS - d, XS)]
        return remote(piece, piece, o_send.at[4, d - 1], o_recv.at[4, d - 1], sibling)

    @pl.when(x > 0)
    def _():
        answer(at_rep(q, 0, y))

    @pl.when(y > 0)
    def _():
        answer(at_rep(q, x, 0))

    @pl.when(q == 1)
    def _():
        answer(partner)

    @pl.when(c == 0)
    def _():
        answer(sibling)

    load_gain.wait()
    lanes = 128
    pieces = width // lanes

    @pl.loop(0, LOADS)
    def _(b):
        tok_load(b).wait()

        @pl.loop(0, block // ROWS)
        def _(r):
            rows = pl.ds(pl.multiple_of(b * block + r * ROWS, ROWS), ROWS)
            sums = [jnp.zeros((ROWS, lanes), F32) for _ in range(4)]
            for m in range(pieces):
                wide = tok[rows, m * lanes : (m + 1) * lanes].astype(F32)
                sums[m % 4] = sums[m % 4] + wide * wide
            total = jnp.sum((sums[0] + sums[1]) + (sums[2] + sums[3]), axis=1, keepdims=True)
            scale = jnp.broadcast_to(lax.rsqrt(total * (1.0 / width) + EPSILON), (ROWS, lanes))
            inv[rows, :] = scale
            for m in range(pieces):
                cols = slice(m * lanes, (m + 1) * lanes)
                nrm[rows, cols] = (tok[rows, cols].astype(F32) * scale * gain[:, cols]).astype(BF16)

    wait_for(here_sem, (1 - x_later) * (XS - 1) + (1 - y_later) * (YS - 1) + (ZS - 1 - q) + c)

    @pl.when(x == 0)
    def _():
        for d in range(1, XS):
            pl.semaphore_signal(all_sem, inc=1, device_id=at_rep(q, d, y), device_id_type=MESH)

    @pl.when(y == 0)
    def _():
        for d in range(1, YS):
            pl.semaphore_signal(all_sem, inc=1, device_id=at_rep(q, x, d), device_id_type=MESH)

    for i in range(CHUNKS):
        own_to_sibling(i).start()

    load_kg.wait()
    upper = z // (CHIPS // 2)

    def cols_of(owner, i):
        return pl.ds(pl.multiple_of(owner * shard + i * part, part), part)

    def terms(owner, i):
        got = lax.dot_general(
            nrm[:, cols_of(owner, i)], kg[...], (((0,), (0,)), ((), ())), preferred_element_type=F32
        )
        buf[P0 + owner, rows_of(i), :] = got.astype(BF16)

    @pl.loop(0, STEPS)
    def _(t):
        n, i = t // CHUNKS, t % CHUNKS
        j = (1 - upper) * (CHIPS - 1 - n) + upper * n

        @pl.loop(0, CORES)
        def _(turn):
            terms(2 * j + lax.rem(o + turn, CORES), i)

            @pl.when(turn == 0)
            def _():
                terms_to_sibling(j, i).start()

    wait_for(all_sem, x_later + y_later)
    for d in range(1, XS):
        x_copy(d).start()

    kacc[...] = jnp.zeros_like(kacc)
    load_w.wait()

    def use_rows(a, core, i):
        owner = 2 * a + core
        rows = buf[W0 + owner, rows_of(i), :]
        cols = cols_of(owner, i)
        kacc[...] += jnp.dot(nrm[:, cols], rows, preferred_element_type=F32)
        d_normed = lax.dot_general(kg[...], rows, (((1,), (1,)), ((), ())), preferred_element_type=F32)
        wide = tok[:, cols].astype(F32)
        for m in range(part // lanes):
            here = slice(m * lanes, (m + 1) * lanes)
            got = jnp.sum(d_normed[:, here] * wide[:, here] * inv[...], axis=0, keepdims=True)
            g_own[core, a, pl.ds(i * (part // lanes) + m, 1), :] = got

    def add_terms(j, i, base, from_line):
        rows = rows_of(i)
        terms_to_sibling(j, i).wait_recv()
        own = buf[P0 + 2 * j + c, rows, :].astype(F32) + buf[S0 + j, rows, :].astype(F32)

        @pl.when(from_line)
        def _():
            buf[P0 + 2 * j + c, rows, :] = (own + buf[base + j, rows, :].astype(F32)).astype(BF16)

        @pl.when(jnp.logical_not(from_line))
        def _():
            buf[P0 + 2 * j + c, rows, :] = own.astype(BF16)

    gain_swap = remote(g_own.at[o], g_sib, g_send.at[0], g_recv.at[0], sibling)

    def gain_copy(d):
        to = lax.rem(z + d, CHIPS)
        return remote(g_own.at[c, to], g_z.at[z], g_send.at[d], g_recv.at[d], at_chip(to))

    def gain_wait(d):
        slot = g_z.at[lax.rem(z + CHIPS - d, CHIPS)]
        return remote(slot, slot, g_send.at[d], g_recv.at[d], sibling)

    def gain_out(d):
        sem = CHIPS + d - 1
        return remote(g_fin.at[z, c], g_fin.at[z, c], g_send.at[sem], g_recv.at[sem], at_chip(lax.rem(z + d, CHIPS)))

    def gain_in(d):
        slot, sem = g_fin.at[lax.rem(z + CHIPS - d, CHIPS), c], CHIPS + d - 1
        return remote(slot, slot, g_send.at[sem], g_recv.at[sem], sibling)

    gain_back = remote(g_fin.at[:, c], g_fin.at[:, c], g_send.at[2 * CHIPS - 1], g_recv.at[2 * CHIPS - 1], sibling)
    gain_back_in = remote(g_fin.at[:, o], g_fin.at[:, o], g_send.at[2 * CHIPS - 1], g_recv.at[2 * CHIPS - 1], sibling)

    @pl.loop(0, STEPS)
    def _(s):
        k, i = s // CHUNKS, s % CHUNKS

        @pl.when(s == 2)
        def _():
            load_lp.wait()
            for d in range(1, XS):
                x_wait(d).wait_recv()
            for m in range(YS):
                cols = slice(m * ycols, (m + 1) * ycols)
                ysum[m] = (xr[0, :, cols].astype(F32) + xr[1, :, cols].astype(F32)) + (
                    xr[2, :, cols].astype(F32) + xr[3, :, cols].astype(F32)
                )
            for d in range(1, YS):
                y_copy(d).start()
            yr[y] = ysum[y]

        @pl.when(s == 4)
        def _():
            for d in range(1, YS):
                y_wait(d).wait_recv()
            load_op.wait()
            cols = pl.ds(pl.multiple_of(x * xcols + y * ycols, ycols), ycols)
            total = (yr[0] + yr[1]) + (yr[2] + yr[3])
            zs[...] = (float(XS * YS) * op[:, cols] - total).astype(BF16)
            z_copy.start()

        @pl.when(s == 9)
        def _():
            z_copy.wait_recv()
            ps[x, y] = (zs[...].astype(F32) + zr[...].astype(F32)) * (1.0 / (XS * YS * ZS))
            for d in range(1, YS):
                y_back(d).start()

        @pl.when(s == 10)
        def _():
            for d in range(1, YS):
                y_back_wait(d).wait_recv()
            for d in range(1, XS):
                x_back(d).start()

        @pl.when(s == STEPS - 2)
        def _():
            for d in range(1, XS):
                x_back_wait(d).wait_recv()
            load_mo.wait()
            load_step.wait()
            rate = OUTER_LR * (step_ref[0].astype(F32) + 1.0) / WARM
            for a in range(XS):
                for b in range(YS):
                    cols = slice((a * YS + b) * ycols, (a * YS + b + 1) * ycols)
                    pseudo = ps[a, b]
                    moment = OUTER_MOMENTUM * mo[:, cols] + pseudo
                    mo[:, cols] = moment
                    op[:, cols] = op[:, cols] - rate * (pseudo + OUTER_MOMENTUM * moment)

        @pl.when(s == LAST + 1)
        def _():
            for d in range(1, CHIPS):
                gain_wait(d).wait_recv()
            g_fin[z, c] = (g_z[0] + g_z[1]) + (g_z[2] + g_z[3])
            for d in range(1, CHIPS):
                gain_out(d).start()

        @pl.when(s == STEPS - 1)
        def _():
            for d in range(1, CHIPS):
                gain_in(d).wait_recv()
            gain_back.start()

        @pl.when(jnp.logical_and(has_right, s > 1))
        def _():
            line_copy(s - 2, True).wait_send()

        @pl.when(jnp.logical_and(has_left, s > 1))
        def _():
            line_copy(s - 2, False).wait_send()

        @pl.when(k == CHIPS - 1)
        def _():
            for a in range(CHIPS):
                to_sibling(a, i).wait_send()
                terms_to_sibling(a, i).wait_send()

        @pl.when(s == LAST + 1)
        def _():
            gain_swap.wait_send()
            for d in range(1, XS):
                x_copy(d).wait_send()
                x_back(d).wait_send()
            for d in range(1, YS):
                y_copy(d).wait_send()
                y_back(d).wait_send()
            z_copy.wait_send()

        @pl.when(s == STEPS - 1)
        def _():
            for d in range(1, CHIPS):
                gain_copy(d).wait_send()
                gain_out(d).wait_send()

        @pl.when(k == CHIPS - 1)
        def _():
            rows = rows_of(i)
            terms_to_sibling(z, i).wait_recv()
            wg[rows, :] = buf[P0 + 2 * z + c, rows, :].astype(F32) + buf[S0 + z, rows, :].astype(F32)

        @pl.when(has_left)
        def _():
            line_copy(s, True).wait_recv()

        @pl.when(has_right)
        def _():
            line_copy(s, False).wait_recv()

        left_weights = jnp.logical_and(has_left, k <= z - 1)
        right_weights = jnp.logical_and(has_right, k <= CHIPS - 2 - z)

        @pl.when(left_weights)
        def _():
            to_sibling(z - 1 - k, i).start()

        @pl.when(right_weights)
        def _():
            to_sibling(z + 1 + k, i).start()

        @pl.loop(0, 3 * CORES)
        def _(t):
            source, turn = t // CORES, t % CORES
            is_left, is_right, is_own = source == 0, source == 1, source == 2
            a = z + (1 + k) * (is_right.astype(jnp.int32) - is_left.astype(jnp.int32))
            have = jnp.logical_or(
                jnp.logical_or(jnp.logical_and(is_left, left_weights), jnp.logical_and(is_right, right_weights)),
                jnp.logical_and(is_own, k == 1),
            )

            @pl.when(jnp.logical_and(have, turn == 1))
            def _():
                from_sibling(a, i).wait_recv()

            @pl.when(have)
            def _():
                use_rows(a, lax.rem(c + turn, CORES), i)

        @pl.when(s == LAST - 1)
        def _():
            gain_swap.start()
            kout[...] = kacc[...].astype(BF16)

        later = k + 1

        @pl.loop(0, 2)
        def _(t):
            to_left = t == 1
            j = later * (2 * t - 1) + CHIPS * (1 - 2 * t) + z
            goes = jnp.logical_or(
                jnp.logical_and(jnp.logical_not(to_left), jnp.logical_and(has_right, later > z)),
                jnp.logical_and(to_left, jnp.logical_and(has_left, later > CHIPS - 1 - z)),
            )
            comes = jnp.logical_or(jnp.logical_and(to_left, has_right), jnp.logical_and(jnp.logical_not(to_left), has_left))

            @pl.when(jnp.logical_and(later < CHIPS, goes))
            def _():
                add_terms(j, i, R0 + (L0 - R0) * t, comes)

        @pl.when(s == LAST - 1)
        def _():
            gain_swap.wait_recv()
            g_own[c] = g_own[c] + g_sib[...]
            for d in range(1, CHIPS):
                gain_copy(d).start()
            g_z[z] = g_own[c, z]

        early, late = s < LAST + 2 - CHUNKS, jnp.logical_and(s >= LAST, s < LAST + 2)
        n = s + CHUNKS - (CHUNKS - 2) * late.astype(jnp.int32)
        due = jnp.logical_or(early, late)

        @pl.when(jnp.logical_and(has_right, due))
        def _():
            line_copy(n, True).start()

        @pl.when(jnp.logical_and(has_left, due))
        def _():
            line_copy(n, False).start()

        @pl.when(k == CHIPS - 1)
        def _():
            rows = rows_of(i)

            @pl.when(jnp.logical_and(has_left, has_right))
            def _():
                wg[rows, :] += buf[R0 + z, rows, :].astype(F32) + buf[L0 + z, rows, :].astype(F32)

            @pl.when(jnp.logical_not(jnp.logical_and(has_left, has_right)))
            def _():
                wg[rows, :] += buf[R0 + z + (L0 - R0) * (1 - has_left.astype(jnp.int32)), rows, :].astype(F32)

    gain_back_in.wait_recv()
    gain_back.wait_send()

    @pl.when(has_right)
    def _():
        line_copy(STEPS - 2, True).wait_send()
        line_copy(STEPS - 1, True).wait_send()

    @pl.when(has_left)
    def _():
        line_copy(STEPS - 2, False).wait_send()
        line_copy(STEPS - 1, False).wait_send()


def write_out(*refs):
    count = len(PIECES)
    results, outs, sems = refs[:count], refs[count : 2 * count], refs[-1]
    writes = []
    for result, out, pieces in zip(results, outs, PIECES):
        size = result.shape[0] // pieces
        for i in range(pieces):
            here = pl.ds(i * size, size)
            writes.append(pltpu.make_async_copy(result.at[here], out.at[here], sems.at[len(writes)]))
    for write in writes:
        write.start()
    for write in writes:
        write.wait()


def local(tokens, key_weight, key_grad, norm_gain, outer_params, local_params, momentum, outer_step):
    rows, width = tokens.shape
    _, shard, kw = key_weight.shape
    frag = outer_params.shape[0]
    xcols, ycols = width // XS, width // XS // YS
    lanes = 128
    dma, anywhere = pltpu.SemaphoreType.DMA, pl.BlockSpec(memory_space=pltpu.HBM)
    results = (
        ((rows, kw), BF16),
        ((shard, kw), F32),
        ((CHIPS, CORES, shard // lanes, lanes), F32),
        (outer_params.shape, F32),
        (momentum.shape, F32),
    )
    held = pl.pallas_call(
        kernel,
        out_shape=tuple(pltpu.VMEM(*result) for result in results),
        in_specs=[anywhere] * 8,
        out_specs=(pl.BlockSpec(memory_space=pltpu.VMEM),) * 5,
        scratch_shapes=[
            pltpu.VMEM((rows, width), BF16),
            pltpu.VMEM((rows, width), BF16),
            pltpu.VMEM((rows, kw), BF16),
            pltpu.VMEM((1, width), F32),
            pltpu.VMEM((rows, lanes), F32),
            pltpu.VMEM((SLOTS, shard, kw), BF16),
            pltpu.VMEM((rows, kw), F32),
            pltpu.VMEM((CORES, CHIPS, shard // lanes, lanes), F32),
            pltpu.VMEM((CHIPS, shard // lanes, lanes), F32),
            pltpu.VMEM((CHIPS, shard // lanes, lanes), F32),
            pltpu.VMEM((XS, frag, xcols), BF16),
            pltpu.VMEM((YS, frag, ycols), F32),
            pltpu.VMEM((YS, frag, ycols), F32),
            pltpu.VMEM((frag, ycols), BF16),
            pltpu.VMEM((frag, ycols), BF16),
            pltpu.VMEM((XS, YS, frag, ycols), F32),
            pltpu.SMEM((1,), jnp.int32),
            dma((LOADS,)),
            dma((7,)),
            dma((STEPS,)),
            dma((STEPS,)),
            dma((STEPS,)),
            dma((STEPS,)),
            dma((CHIPS, CHUNKS)),
            dma((CHIPS, CHUNKS)),
            dma((CHIPS, CHUNKS)),
            dma((CHIPS, CHUNKS)),
            dma((2 * CHIPS,)),
            dma((2 * CHIPS,)),
            dma((5, 3)),
            dma((5, 3)),
            pltpu.SemaphoreType.REGULAR,
            pltpu.SemaphoreType.REGULAR,
            pltpu.SemaphoreType.REGULAR,
        ],
        compiler_params=pltpu.CompilerParams(
            collective_id=0, has_side_effects=True, vmem_limit_bytes=54 * MIB
        ),
        cost_estimate=pl.CostEstimate(
            flops=6 * rows * width * kw, bytes_accessed=16 * MIB, transcendentals=rows
        ),
        name="outer_and_keys",
    )(
        tokens, key_weight[0], key_grad, norm_gain, outer_params, local_params[0], momentum, outer_step
    )
    keys, weight_grad, gain_grad, new_outer, new_momentum = pl.pallas_call(
        write_out,
        out_shape=tuple(jax.ShapeDtypeStruct(*result) for result in results),
        in_specs=[pl.BlockSpec(memory_space=pltpu.VMEM)] * len(results),
        out_specs=(anywhere,) * len(results),
        scratch_shapes=[dma((sum(PIECES),))],
        compiler_params=pltpu.CompilerParams(vmem_limit_bytes=MIB),
        name="write_out",
    )(*[pltpu.with_memory_space_constraint(a, pltpu.VMEM) for a in held])
    return keys, weight_grad[None], gain_grad.reshape(1, width), new_outer, new_momentum


def solution(mesh):
    placed = (
        P(("rep", "fsdp"), None),
        P("rep", "fsdp", None),
        P(("rep", "fsdp"), None),
        P("rep", None),
        P("fsdp", None),
        P("rep", "fsdp", None),
        P("fsdp", None),
        P(),
    )
    return jax.shard_map(
        local,
        mesh=mesh,
        in_specs=placed,
        out_specs=(
            P(("rep", "fsdp"), None),
            P("rep", "fsdp", None),
            P("rep", None),
            P("fsdp", None),
            P("fsdp", None),
        ),
        check_vma=False,
    )
```

```python
import functools

import jax
import jax.numpy as jnp
from jax import lax
from jax.experimental import pallas as pl
from jax.experimental.pallas import tpu as pltpu
from jax.sharding import PartitionSpec as P

MESH = pl.DeviceIdType.MESH
BF16, F32 = jnp.bfloat16, jnp.float32

WARM = 8
EPSILON = 1e-05
OUTER_LR = 0.7
OUTER_MOMENTUM = 0.9

CHIPS, CORES = 4, 2
XS, YS, ZS = 4, 4, 2
CHUNKS = 4
STEPS = CHIPS * CHUNKS
LAST = STEPS - CHUNKS
LOADS = 6
ROWS = 16
PIECES = (1, 1, 1, 1, 1)
MIB = 1024 * 1024

W0, P0, S0, R0, L0 = 0, 8, 16, 20, 24
SLOTS = 28


def kernel(
    tok_hbm, kw_hbm, kg_hbm, gain_hbm, op_hbm, lp_hbm, mo_hbm, step_hbm,
    kout, wg, g_fin, op, mo,
    tok, nrm, kg, gain, inv, buf, kacc,
    g_own, g_sib, g_z,
    xr, ysum, yr, zs, zr, ps,
    step_ref, tok_sem, ld_sem,
    r_send, r_recv, l_send, l_recv,
    w_send, w_recv, p_send, p_recv,
    g_send, g_recv, o_send, o_recv, here_sem, line_sem, all_sem,
):
    tokens, width = tok.shape
    shard, kw = buf.shape[1:]
    part = shard // CHUNKS
    frag = op.shape[0]
    xcols, ycols = width // XS, width // XS // YS

    rep, fsdp = lax.axis_index("rep"), lax.axis_index("fsdp")
    q, x, y = rep // (XS * YS), (rep // YS) % XS, rep % YS
    z, c = fsdp // CORES, fsdp % CORES
    o = 1 - c

    def at_rep(q_, x_, y_):
        return ((q_ * XS + x_) * YS + y_, fsdp)

    def at_chip(z_):
        return (rep, z_ * CORES + c)

    sibling = (rep, z * CORES + o)
    right, left = at_chip(lax.rem(z + 1, CHIPS)), at_chip(lax.rem(z + CHIPS - 1, CHIPS))
    has_right, has_left = z < CHIPS - 1, z > 0

    def remote(src, dst, send, recv, device):
        return pltpu.make_async_remote_copy(
            src_ref=src, dst_ref=dst, send_sem=send, recv_sem=recv, device_id=device, device_id_type=MESH
        )

    def rows_of(i):
        return pl.ds(pl.multiple_of(i * part, part), part)

    barrier = pltpu.get_barrier_semaphore()
    partner = at_rep(1 - q, x, y)

    def greet(peer):
        pl.semaphore_signal(barrier, inc=1, device_id=peer, device_id_type=MESH)

    def answer(peer):
        pl.semaphore_signal(here_sem, inc=1, device_id=peer, device_id_type=MESH)

    def wait_for(sem, count):
        @pl.when(count > 0)
        def _():
            pl.semaphore_wait(sem, count)

    both = jnp.logical_and(has_right, q == 1)

    @pl.when(q == 0)
    def _():
        greet(partner)

    @pl.when(has_right)
    def _():
        greet(right)

    @pl.when(jnp.logical_and(has_left, q == 1))
    def _():
        greet(left)

    @pl.when(c == 1)
    def _():
        greet(sibling)

    @pl.when(x == 0)
    def _():
        for d in range(1, XS):
            greet(at_rep(q, d, y))

    @pl.when(y == 0)
    def _():
        for d in range(1, YS):
            greet(at_rep(q, x, d))

    x_later, y_later = (x > 0).astype(jnp.int32), (y > 0).astype(jnp.int32)
    wait_for(barrier, has_left.astype(jnp.int32) + both.astype(jnp.int32) + o + x_later + y_later + q)

    @pl.when(jnp.logical_and(has_left, q == 0))
    def _():
        pl.semaphore_signal(line_sem, inc=1, device_id=left, device_id_type=MESH)

    block = tokens // LOADS

    def tok_load(b):
        rows = pl.ds(pl.multiple_of(b * block, block), block)
        return pltpu.make_async_copy(tok_hbm.at[rows], tok.at[rows], tok_sem.at[b])

    load_gain = pltpu.make_async_copy(gain_hbm, gain, ld_sem.at[0])
    load_kg = pltpu.make_async_copy(kg_hbm, kg, ld_sem.at[1])
    load_w = pltpu.make_async_copy(kw_hbm, buf.at[W0 + 2 * z + c], ld_sem.at[2])
    own_x = pl.ds(pl.multiple_of(x * xcols, xcols), xcols)
    load_lp = pltpu.make_async_copy(lp_hbm.at[:, own_x], xr.at[x], ld_sem.at[3])
    load_op = pltpu.make_async_copy(op_hbm, op, ld_sem.at[4])
    load_mo = pltpu.make_async_copy(mo_hbm, mo, ld_sem.at[5])
    load_step = pltpu.make_async_copy(step_hbm, step_ref, ld_sem.at[6])

    def line_first(n, rightward):
        rows = rows_of(n)
        dst = buf.at[W0 + 2 * z + c, rows]
        if rightward:
            return remote(kw_hbm.at[rows], dst, r_send.at[n], r_recv.at[n], right)
        return remote(kw_hbm.at[rows], dst, l_send.at[n], l_recv.at[n], left)

    def line_copy(n, rightward):
        k, rows = n // CHUNKS, rows_of(n % CHUNKS)
        if rightward:
            is_sum = (k - z + CHIPS - 1) // CHIPS
            weight, owner = 2 * (z - k) + c, CHIPS + z - k
            src = (1 - is_sum) * (W0 + weight) + is_sum * (P0 + 2 * owner + c)
            dst = (1 - is_sum) * (W0 + weight) + is_sum * (R0 + owner)
            return remote(buf.at[src, rows], buf.at[dst, rows], r_send.at[n], r_recv.at[n], right)
        is_sum = (k + z) // CHIPS
        weight, owner = 2 * (z + k) + c, k + z - CHIPS
        src = (1 - is_sum) * (W0 + weight) + is_sum * (P0 + 2 * owner + c)
        dst = (1 - is_sum) * (W0 + weight) + is_sum * (L0 + owner)
        return remote(buf.at[src, rows], buf.at[dst, rows], l_send.at[n], l_recv.at[n], left)

    @pl.when(has_left)
    def _():
        for n in range(CHUNKS):
            line_first(n, False).start()

    @pl.when(jnp.logical_and(has_right, q == 0))
    def _():
        pl.semaphore_wait(line_sem, 1)

    @pl.when(has_right)
    def _():
        for n in range(CHUNKS):
            line_first(n, True).start()

    load_gain.start()
    tok_load(0).start()
    load_kg.start()
    for b in range(1, LOADS):
        tok_load(b).start()
    for load in (load_w, load_lp, load_op, load_mo, load_step):
        load.start()

    def own_to_sibling(i):
        rows = rows_of(i)
        return remote(
            kw_hbm.at[rows], buf.at[W0 + 2 * z + c, rows], w_send.at[z, i], w_recv.at[z, i], sibling
        )

    def to_sibling(a, i):
        there = buf.at[W0 + 2 * a + c, rows_of(i)]
        return remote(there, there, w_send.at[a, i], w_recv.at[a, i], sibling)

    def from_sibling(a, i):
        there = buf.at[W0 + 2 * a + o, rows_of(i)]
        return remote(there, there, w_send.at[a, i], w_recv.at[a, i], sibling)

    def terms_to_sibling(j, i):
        return remote(
            buf.at[P0 + 2 * j + o, rows_of(i)], buf.at[S0 + j, rows_of(i)], p_send.at[j, i], p_recv.at[j, i], sibling
        )

    def x_copy(d):
        to = lax.rem(x + d, XS)
        cols = pl.ds(pl.multiple_of(to * xcols, xcols), xcols)
        return remote(lp_hbm.at[:, cols], xr.at[x], o_send.at[0, d - 1], o_recv.at[0, d - 1], at_rep(q, to, y))

    def x_wait(d):
        slot = xr.at[lax.rem(x + XS - d, XS)]
        return remote(slot, slot, o_send.at[0, d - 1], o_recv.at[0, d - 1], sibling)

    def y_copy(d):
        to = lax.rem(y + d, YS)
        return remote(ysum.at[to], yr.at[y], o_send.at[1, d - 1], o_recv.at[1, d - 1], at_rep(q, x, to))

    def y_wait(d):
        slot = yr.at[lax.rem(y + YS - d, YS)]
        return remote(slot, slot, o_send.at[1, d - 1], o_recv.at[1, d - 1], sibling)

    z_copy = remote(zs, zr, o_send.at[2, 0], o_recv.at[2, 0], partner)

    def y_back(d):
        piece = ps.at[x, y]
        return remote(
            piece, piece, o_send.at[3, d - 1], o_recv.at[3, d - 1], at_rep(q, x, lax.rem(y + d, YS))
        )

    def y_back_wait(d):
        piece = ps.at[x, lax.rem(y + YS - d, YS)]
        return remote(piece, piece, o_send.at[3, d - 1], o_recv.at[3, d - 1], sibling)

    def x_back(d):
        piece = ps.at[x]
        return remote(
            piece, piece, o_send.at[4, d - 1], o_recv.at[4, d - 1], at_rep(q, lax.rem(x + d, XS), y)
        )

    def x_back_wait(d):
        piece = ps.at[lax.rem(x + XS - d, XS)]
        return remote(piece, piece, o_send.at[4, d - 1], o_recv.at[4, d - 1], sibling)

    @pl.when(x > 0)
    def _():
        answer(at_rep(q, 0, y))

    @pl.when(y > 0)
    def _():
        answer(at_rep(q, x, 0))

    @pl.when(q == 1)
    def _():
        answer(partner)

    @pl.when(c == 0)
    def _():
        answer(sibling)

    load_gain.wait()
    lanes = 128
    pieces = width // lanes

    @pl.loop(0, LOADS)
    def _(b):
        tok_load(b).wait()

        @pl.loop(0, block // ROWS)
        def _(r):
            rows = pl.ds(pl.multiple_of(b * block + r * ROWS, ROWS), ROWS)
            sums = [jnp.zeros((ROWS, lanes), F32) for _ in range(4)]
            for m in range(pieces):
                wide = tok[rows, m * lanes : (m + 1) * lanes].astype(F32)
                sums[m % 4] = sums[m % 4] + wide * wide
            total = jnp.sum((sums[0] + sums[1]) + (sums[2] + sums[3]), axis=1, keepdims=True)
            scale = jnp.broadcast_to(lax.rsqrt(total * (1.0 / width) + EPSILON), (ROWS, lanes))
            inv[rows, :] = scale
            for m in range(pieces):
                cols = slice(m * lanes, (m + 1) * lanes)
                nrm[rows, cols] = (tok[rows, cols].astype(F32) * scale * gain[:, cols]).astype(BF16)

    wait_for(here_sem, (1 - x_later) * (XS - 1) + (1 - y_later) * (YS - 1) + (ZS - 1 - q) + c)

    @pl.when(x == 0)
    def _():
        for d in range(1, XS):
            pl.semaphore_signal(all_sem, inc=1, device_id=at_rep(q, d, y), device_id_type=MESH)

    @pl.when(y == 0)
    def _():
        for d in range(1, YS):
            pl.semaphore_signal(all_sem, inc=1, device_id=at_rep(q, x, d), device_id_type=MESH)

    for i in range(CHUNKS):
        own_to_sibling(i).start()

    load_kg.wait()
    upper = z // (CHIPS // 2)

    def cols_of(owner, i):
        return pl.ds(pl.multiple_of(owner * shard + i * part, part), part)

    def terms(owner, i):
        got = lax.dot_general(
            nrm[:, cols_of(owner, i)], kg[...], (((0,), (0,)), ((), ())), preferred_element_type=F32
        )
        buf[P0 + owner, rows_of(i), :] = got.astype(BF16)

    @pl.loop(0, STEPS)
    def _(t):
        n, i = t // CHUNKS, t % CHUNKS
        j = (1 - upper) * (CHIPS - 1 - n) + upper * n

        @pl.loop(0, CORES)
        def _(turn):
            terms(2 * j + lax.rem(o + turn, CORES), i)

            @pl.when(turn == 0)
            def _():
                terms_to_sibling(j, i).start()

    wait_for(all_sem, x_later + y_later)
    for d in range(1, XS):
        x_copy(d).start()

    kacc[...] = jnp.zeros_like(kacc)
    load_w.wait()

    def use_rows(a, core, i):
        owner = 2 * a + core
        rows = buf[W0 + owner, rows_of(i), :]
        cols = cols_of(owner, i)
        kacc[...] += jnp.dot(nrm[:, cols], rows, preferred_element_type=F32)
        d_normed = lax.dot_general(kg[...], rows, (((1,), (1,)), ((), ())), preferred_element_type=F32)
        wide = tok[:, cols].astype(F32)
        for m in range(part // lanes):
            here = slice(m * lanes, (m + 1) * lanes)
            got = jnp.sum(d_normed[:, here] * wide[:, here] * inv[...], axis=0, keepdims=True)
            g_own[core, a, pl.ds(i * (part // lanes) + m, 1), :] = got

    def add_terms(j, i, base, from_line):
        rows = rows_of(i)
        terms_to_sibling(j, i).wait_recv()
        own = buf[P0 + 2 * j + c, rows, :].astype(F32) + buf[S0 + j, rows, :].astype(F32)

        @pl.when(from_line)
        def _():
            buf[P0 + 2 * j + c, rows, :] = (own + buf[base + j, rows, :].astype(F32)).astype(BF16)

        @pl.when(jnp.logical_not(from_line))
        def _():
            buf[P0 + 2 * j + c, rows, :] = own.astype(BF16)

    gain_swap = remote(g_own.at[o], g_sib, g_send.at[0], g_recv.at[0], sibling)

    def gain_copy(d):
        to = lax.rem(z + d, CHIPS)
        return remote(g_own.at[c, to], g_z.at[z], g_send.at[d], g_recv.at[d], at_chip(to))

    def gain_wait(d):
        slot = g_z.at[lax.rem(z + CHIPS - d, CHIPS)]
        return remote(slot, slot, g_send.at[d], g_recv.at[d], sibling)

    def gain_out(d):
        sem = CHIPS + d - 1
        return remote(g_fin.at[z, c], g_fin.at[z, c], g_send.at[sem], g_recv.at[sem], at_chip(lax.rem(z + d, CHIPS)))

    def gain_in(d):
        slot, sem = g_fin.at[lax.rem(z + CHIPS - d, CHIPS), c], CHIPS + d - 1
        return remote(slot, slot, g_send.at[sem], g_recv.at[sem], sibling)

    gain_back = remote(g_fin.at[:, c], g_fin.at[:, c], g_send.at[2 * CHIPS - 1], g_recv.at[2 * CHIPS - 1], sibling)
    gain_back_in = remote(g_fin.at[:, o], g_fin.at[:, o], g_send.at[2 * CHIPS - 1], g_recv.at[2 * CHIPS - 1], sibling)

    @pl.loop(0, STEPS)
    def _(s):
        k, i = s // CHUNKS, s % CHUNKS

        @pl.when(s == 2)
        def _():
            load_lp.wait()
            for d in range(1, XS):
                x_wait(d).wait_recv()
            for m in range(YS):
                cols = slice(m * ycols, (m + 1) * ycols)
                ysum[m] = (xr[0, :, cols].astype(F32) + xr[1, :, cols].astype(F32)) + (
                    xr[2, :, cols].astype(F32) + xr[3, :, cols].astype(F32)
                )
            for d in range(1, YS):
                y_copy(d).start()
            yr[y] = ysum[y]

        @pl.when(s == 4)
        def _():
            for d in range(1, YS):
                y_wait(d).wait_recv()
            load_op.wait()
            cols = pl.ds(pl.multiple_of(x * xcols + y * ycols, ycols), ycols)
            total = (yr[0] + yr[1]) + (yr[2] + yr[3])
            zs[...] = (float(XS * YS) * op[:, cols] - total).astype(BF16)
            z_copy.start()

        @pl.when(s == 9)
        def _():
            z_copy.wait_recv()
            ps[x, y] = (zs[...].astype(F32) + zr[...].astype(F32)) * (1.0 / (XS * YS * ZS))
            for d in range(1, YS):
                y_back(d).start()

        @pl.when(s == 10)
        def _():
            for d in range(1, YS):
                y_back_wait(d).wait_recv()
            for d in range(1, XS):
                x_back(d).start()

        @pl.when(s == STEPS - 2)
        def _():
            for d in range(1, XS):
                x_back_wait(d).wait_recv()
            load_mo.wait()
            load_step.wait()
            rate = OUTER_LR * (step_ref[0].astype(F32) + 1.0) / WARM
            for a in range(XS):
                for b in range(YS):
                    cols = slice((a * YS + b) * ycols, (a * YS + b + 1) * ycols)
                    pseudo = ps[a, b]
                    moment = OUTER_MOMENTUM * mo[:, cols] + pseudo
                    mo[:, cols] = moment
                    op[:, cols] = op[:, cols] - rate * (pseudo + OUTER_MOMENTUM * moment)

        @pl.when(s == LAST + 1)
        def _():
            for d in range(1, CHIPS):
                gain_wait(d).wait_recv()
            g_fin[z, c] = (g_z[0] + g_z[1]) + (g_z[2] + g_z[3])
            for d in range(1, CHIPS):
                gain_out(d).start()

        @pl.when(s == STEPS - 1)
        def _():
            for d in range(1, CHIPS):
                gain_in(d).wait_recv()
            gain_back.start()

        @pl.when(jnp.logical_and(has_right, s > 1))
        def _():
            line_copy(s - 2, True).wait_send()

        @pl.when(jnp.logical_and(has_left, s > 1))
        def _():
            line_copy(s - 2, False).wait_send()

        @pl.when(k == CHIPS - 1)
        def _():
            for a in range(CHIPS):
                to_sibling(a, i).wait_send()
                terms_to_sibling(a, i).wait_send()

        @pl.when(s == LAST + 1)
        def _():
            gain_swap.wait_send()
            for d in range(1, XS):
                x_copy(d).wait_send()
                x_back(d).wait_send()
            for d in range(1, YS):
                y_copy(d).wait_send()
                y_back(d).wait_send()
            z_copy.wait_send()

        @pl.when(s == STEPS - 1)
        def _():
            for d in range(1, CHIPS):
                gain_copy(d).wait_send()
                gain_out(d).wait_send()

        @pl.when(k == CHIPS - 1)
        def _():
            rows = rows_of(i)
            terms_to_sibling(z, i).wait_recv()
            wg[rows, :] = buf[P0 + 2 * z + c, rows, :].astype(F32) + buf[S0 + z, rows, :].astype(F32)

        @pl.when(has_left)
        def _():
            line_copy(s, True).wait_recv()

        @pl.when(has_right)
        def _():
            line_copy(s, False).wait_recv()

        left_weights = jnp.logical_and(has_left, k <= z - 1)
        right_weights = jnp.logical_and(has_right, k <= CHIPS - 2 - z)

        @pl.when(left_weights)
        def _():
            to_sibling(z - 1 - k, i).start()

        @pl.when(right_weights)
        def _():
            to_sibling(z + 1 + k, i).start()

        @pl.loop(0, 3 * CORES)
        def _(t):
            source, turn = t // CORES, t % CORES
            is_left, is_right, is_own = source == 0, source == 1, source == 2
            a = z + (1 + k) * (is_right.astype(jnp.int32) - is_left.astype(jnp.int32))
            have = jnp.logical_or(
                jnp.logical_or(jnp.logical_and(is_left, left_weights), jnp.logical_and(is_right, right_weights)),
                jnp.logical_and(is_own, k == 1),
            )

            @pl.when(jnp.logical_and(have, turn == 1))
            def _():
                from_sibling(a, i).wait_recv()

            @pl.when(have)
            def _():
                use_rows(a, lax.rem(c + turn, CORES), i)

        @pl.when(s == LAST - 1)
        def _():
            gain_swap.start()
            kout[...] = kacc[...].astype(BF16)

        later = k + 1

        @pl.loop(0, 2)
        def _(t):
            to_left = t == 1
            j = later * (2 * t - 1) + CHIPS * (1 - 2 * t) + z
            goes = jnp.logical_or(
                jnp.logical_and(jnp.logical_not(to_left), jnp.logical_and(has_right, later > z)),
                jnp.logical_and(to_left, jnp.logical_and(has_left, later > CHIPS - 1 - z)),
            )
            comes = jnp.logical_or(jnp.logical_and(to_left, has_right), jnp.logical_and(jnp.logical_not(to_left), has_left))

            @pl.when(jnp.logical_and(later < CHIPS, goes))
            def _():
                add_terms(j, i, R0 + (L0 - R0) * t, comes)

        @pl.when(s == LAST - 1)
        def _():
            gain_swap.wait_recv()
            g_own[c] = g_own[c] + g_sib[...]
            for d in range(1, CHIPS):
                gain_copy(d).start()
            g_z[z] = g_own[c, z]

        early, late = s < LAST + 2 - CHUNKS, jnp.logical_and(s >= LAST, s < LAST + 2)
        n = s + CHUNKS - (CHUNKS - 2) * late.astype(jnp.int32)
        due = jnp.logical_or(early, late)

        @pl.when(jnp.logical_and(has_right, due))
        def _():
            line_copy(n, True).start()

        @pl.when(jnp.logical_and(has_left, due))
        def _():
            line_copy(n, False).start()

        @pl.when(k == CHIPS - 1)
        def _():
            rows = rows_of(i)

            @pl.when(jnp.logical_and(has_left, has_right))
            def _():
                wg[rows, :] += buf[R0 + z, rows, :].astype(F32) + buf[L0 + z, rows, :].astype(F32)

            @pl.when(jnp.logical_not(jnp.logical_and(has_left, has_right)))
            def _():
                wg[rows, :] += buf[R0 + z + (L0 - R0) * (1 - has_left.astype(jnp.int32)), rows, :].astype(F32)

    gain_back_in.wait_recv()
    gain_back.wait_send()

    @pl.when(has_right)
    def _():
        line_copy(STEPS - 2, True).wait_send()
        line_copy(STEPS - 1, True).wait_send()

    @pl.when(has_left)
    def _():
        line_copy(STEPS - 2, False).wait_send()
        line_copy(STEPS - 1, False).wait_send()


def write_out(*refs):
    count = len(PIECES)
    results, outs, sems = refs[:count], refs[count : 2 * count], refs[-1]
    writes = []
    for result, out, pieces in zip(results, outs, PIECES):
        size = result.shape[0] // pieces
        for i in range(pieces):
            here = pl.ds(i * size, size)
            writes.append(pltpu.make_async_copy(result.at[here], out.at[here], sems.at[len(writes)]))
    for write in writes:
        write.start()
    for write in writes:
        write.wait()


def local(tokens, key_weight, key_grad, norm_gain, outer_params, local_params, momentum, outer_step):
    rows, width = tokens.shape
    _, shard, kw = key_weight.shape
    frag = outer_params.shape[0]
    xcols, ycols = width // XS, width // XS // YS
    lanes = 128
    dma, anywhere = pltpu.SemaphoreType.DMA, pl.BlockSpec(memory_space=pltpu.HBM)
    results = (
        ((rows, kw), BF16),
        ((shard, kw), F32),
        ((CHIPS, CORES, shard // lanes, lanes), F32),
        (outer_params.shape, F32),
        (momentum.shape, F32),
    )
    held = pl.pallas_call(
        kernel,
        out_shape=tuple(pltpu.VMEM(*result) for result in results),
        in_specs=[anywhere] * 8,
        out_specs=(pl.BlockSpec(memory_space=pltpu.VMEM),) * 5,
        scratch_shapes=[
            pltpu.VMEM((rows, width), BF16),
            pltpu.VMEM((rows, width), BF16),
            pltpu.VMEM((rows, kw), BF16),
            pltpu.VMEM((1, width), F32),
            pltpu.VMEM((rows, lanes), F32),
            pltpu.VMEM((SLOTS, shard, kw), BF16),
            pltpu.VMEM((rows, kw), F32),
            pltpu.VMEM((CORES, CHIPS, shard // lanes, lanes), F32),
            pltpu.VMEM((CHIPS, shard // lanes, lanes), F32),
            pltpu.VMEM((CHIPS, shard // lanes, lanes), F32),
            pltpu.VMEM((XS, frag, xcols), BF16),
            pltpu.VMEM((YS, frag, ycols), F32),
            pltpu.VMEM((YS, frag, ycols), F32),
            pltpu.VMEM((frag, ycols), BF16),
            pltpu.VMEM((frag, ycols), BF16),
            pltpu.VMEM((XS, YS, frag, ycols), F32),
            pltpu.SMEM((1,), jnp.int32),
            dma((LOADS,)),
            dma((7,)),
            dma((STEPS,)),
            dma((STEPS,)),
            dma((STEPS,)),
            dma((STEPS,)),
            dma((CHIPS, CHUNKS)),
            dma((CHIPS, CHUNKS)),
            dma((CHIPS, CHUNKS)),
            dma((CHIPS, CHUNKS)),
            dma((2 * CHIPS,)),
            dma((2 * CHIPS,)),
            dma((5, 3)),
            dma((5, 3)),
            pltpu.SemaphoreType.REGULAR,
            pltpu.SemaphoreType.REGULAR,
            pltpu.SemaphoreType.REGULAR,
        ],
        compiler_params=pltpu.CompilerParams(
            collective_id=0, has_side_effects=True, vmem_limit_bytes=54 * MIB
        ),
        cost_estimate=pl.CostEstimate(
            flops=6 * rows * width * kw, bytes_accessed=16 * MIB, transcendentals=rows
        ),
        name="outer_and_keys",
    )(
        tokens, key_weight[0], key_grad, norm_gain, outer_params, local_params[0], momentum, outer_step
    )
    keys, weight_grad, gain_grad, new_outer, new_momentum = pl.pallas_call(
        write_out,
        out_shape=tuple(jax.ShapeDtypeStruct(*result) for result in results),
        in_specs=[pl.BlockSpec(memory_space=pltpu.VMEM)] * len(results),
        out_specs=(anywhere,) * len(results),
        scratch_shapes=[dma((sum(PIECES),))],
        compiler_params=pltpu.CompilerParams(vmem_limit_bytes=MIB),
        name="write_out",
    )(*[pltpu.with_memory_space_constraint(a, pltpu.VMEM) for a in held])
    return keys, weight_grad[None], gain_grad.reshape(1, width), new_outer, new_momentum


def solution(mesh):
    placed = (
        P(("rep", "fsdp"), None),
        P("rep", "fsdp", None),
        P(("rep", "fsdp"), None),
        P("rep", None),
        P("fsdp", None),
        P("rep", "fsdp", None),
        P("fsdp", None),
        P(),
    )
    return jax.shard_map(
        local,
        mesh=mesh,
        in_specs=placed,
        out_specs=(
            P(("rep", "fsdp"), None),
            P("rep", "fsdp", None),
            P("rep", None),
            P("fsdp", None),
            P("fsdp", None),
        ),
        check_vma=False,
    )
```

```python
import functools

import jax
import jax.numpy as jnp
from jax import lax
from jax.experimental import pallas as pl
from jax.experimental.pallas import tpu as pltpu
from jax.sharding import PartitionSpec as P

MESH = pl.DeviceIdType.MESH
BF16, F32 = jnp.bfloat16, jnp.float32

WARM = 8
EPSILON = 1e-05
OUTER_LR = 0.7
OUTER_MOMENTUM = 0.9

CHIPS, CORES = 4, 2
XS, YS, ZS = 4, 4, 2
CHUNKS = 4
STEPS = CHIPS * CHUNKS
LAST = STEPS - CHUNKS
LOADS = 6
ROWS = 16
PIECES = (1, 1, 1, 1, 1)
MIB = 1024 * 1024

W0, P0, S0, R0, L0 = 0, 8, 16, 20, 24
SLOTS = 28


def kernel(
    tok_hbm, kw_hbm, kg_hbm, gain_hbm, op_hbm, lp_hbm, mo_hbm, step_hbm,
    kout, wg, g_fin, op, mo,
    tok, nrm, kg, gain, inv, buf, kacc,
    g_own, g_sib, g_z,
    xr, ysum, yr, zs, zr, ps,
    step_ref, tok_sem, ld_sem,
    r_send, r_recv, l_send, l_recv,
    w_send, w_recv, p_send, p_recv,
    g_send, g_recv, o_send, o_recv, here_sem, line_sem, all_sem,
):
    tokens, width = tok.shape
    shard, kw = buf.shape[1:]
    part = shard // CHUNKS
    frag = op.shape[0]
    xcols, ycols = width // XS, width // XS // YS

    rep, fsdp = lax.axis_index("rep"), lax.axis_index("fsdp")
    q, x, y = rep // (XS * YS), (rep // YS) % XS, rep % YS
    z, c = fsdp // CORES, fsdp % CORES
    o = 1 - c

    def at_rep(q_, x_, y_):
        return ((q_ * XS + x_) * YS + y_, fsdp)

    def at_chip(z_):
        return (rep, z_ * CORES + c)

    sibling = (rep, z * CORES + o)
    right, left = at_chip(lax.rem(z + 1, CHIPS)), at_chip(lax.rem(z + CHIPS - 1, CHIPS))
    has_right, has_left = z < CHIPS - 1, z > 0

    def remote(src, dst, send, recv, device):
        return pltpu.make_async_remote_copy(
            src_ref=src, dst_ref=dst, send_sem=send, recv_sem=recv, device_id=device, device_id_type=MESH
        )

    def rows_of(i):
        return pl.ds(pl.multiple_of(i * part, part), part)

    barrier = pltpu.get_barrier_semaphore()
    partner = at_rep(1 - q, x, y)

    def greet(peer):
        pl.semaphore_signal(barrier, inc=1, device_id=peer, device_id_type=MESH)

    def answer(peer):
        pl.semaphore_signal(here_sem, inc=1, device_id=peer, device_id_type=MESH)

    def wait_for(sem, count):
        @pl.when(count > 0)
        def _():
            pl.semaphore_wait(sem, count)

    both = jnp.logical_and(has_right, q == 1)

    @pl.when(q == 0)
    def _():
        greet(partner)

    @pl.when(has_right)
    def _():
        greet(right)

    @pl.when(jnp.logical_and(has_left, q == 1))
    def _():
        greet(left)

    @pl.when(c == 1)
    def _():
        greet(sibling)

    @pl.when(x == 0)
    def _():
        greet(at_rep(q, 1, y))
        greet(at_rep(q, 3, y))

    @pl.when(x == 1)
    def _():
        greet(at_rep(q, 2, y))

    @pl.when(y == 0)
    def _():
        greet(at_rep(q, x, 1))
        greet(at_rep(q, x, 3))

    @pl.when(y == 1)
    def _():
        greet(at_rep(q, x, 2))

    x_later, y_later = (x > 0).astype(jnp.int32), (y > 0).astype(jnp.int32)
    wait_for(barrier, has_left.astype(jnp.int32) + both.astype(jnp.int32) + o + x_later + y_later + q)

    @pl.when(jnp.logical_and(has_left, q == 0))
    def _():
        pl.semaphore_signal(line_sem, inc=1, device_id=left, device_id_type=MESH)

    block = tokens // LOADS

    def tok_load(b):
        rows = pl.ds(pl.multiple_of(b * block, block), block)
        return pltpu.make_async_copy(tok_hbm.at[rows], tok.at[rows], tok_sem.at[b])

    load_gain = pltpu.make_async_copy(gain_hbm, gain, ld_sem.at[0])
    load_kg = pltpu.make_async_copy(kg_hbm, kg, ld_sem.at[1])
    load_w = pltpu.make_async_copy(kw_hbm, buf.at[W0 + 2 * z + c], ld_sem.at[2])
    own_x = pl.ds(pl.multiple_of(x * xcols, xcols), xcols)
    load_lp = pltpu.make_async_copy(lp_hbm.at[:, own_x], xr.at[x], ld_sem.at[3])
    load_op = pltpu.make_async_copy(op_hbm, op, ld_sem.at[4])
    load_mo = pltpu.make_async_copy(mo_hbm, mo, ld_sem.at[5])
    load_step = pltpu.make_async_copy(step_hbm, step_ref, ld_sem.at[6])

    def line_first(n, rightward):
        rows = rows_of(n)
        dst = buf.at[W0 + 2 * z + c, rows]
        if rightward:
            return remote(kw_hbm.at[rows], dst, r_send.at[n], r_recv.at[n], right)
        return remote(kw_hbm.at[rows], dst, l_send.at[n], l_recv.at[n], left)

    def line_copy(n, rightward):
        k, rows = n // CHUNKS, rows_of(n % CHUNKS)
        if rightward:
            is_sum = (k - z + CHIPS - 1) // CHIPS
            weight, owner = 2 * (z - k) + c, CHIPS + z - k
            src = (1 - is_sum) * (W0 + weight) + is_sum * (P0 + 2 * owner + c)
            dst = (1 - is_sum) * (W0 + weight) + is_sum * (R0 + owner)
            return remote(buf.at[src, rows], buf.at[dst, rows], r_send.at[n], r_recv.at[n], right)
        is_sum = (k + z) // CHIPS
        weight, owner = 2 * (z + k) + c, k + z - CHIPS
        src = (1 - is_sum) * (W0 + weight) + is_sum * (P0 + 2 * owner + c)
        dst = (1 - is_sum) * (W0 + weight) + is_sum * (L0 + owner)
        return remote(buf.at[src, rows], buf.at[dst, rows], l_send.at[n], l_recv.at[n], left)

    @pl.when(has_left)
    def _():
        for n in range(CHUNKS):
            line_first(n, False).start()

    @pl.when(jnp.logical_and(has_right, q == 0))
    def _():
        pl.semaphore_wait(line_sem, 1)

    @pl.when(has_right)
    def _():
        for n in range(CHUNKS):
            line_first(n, True).start()

    load_gain.start()
    tok_load(0).start()
    load_kg.start()
    for b in range(1, LOADS):
        tok_load(b).start()
    for load in (load_w, load_lp, load_op, load_mo, load_step):
        load.start()

    def own_to_sibling(i):
        rows = rows_of(i)
        return remote(
            kw_hbm.at[rows], buf.at[W0 + 2 * z + c, rows], w_send.at[z, i], w_recv.at[z, i], sibling
        )

    def to_sibling(a, i):
        there = buf.at[W0 + 2 * a + c, rows_of(i)]
        return remote(there, there, w_send.at[a, i], w_recv.at[a, i], sibling)

    def from_sibling(a, i):
        there = buf.at[W0 + 2 * a + o, rows_of(i)]
        return remote(there, there, w_send.at[a, i], w_recv.at[a, i], sibling)

    def terms_to_sibling(j, i):
        return remote(
            buf.at[P0 + 2 * j + o, rows_of(i)], buf.at[S0 + j, rows_of(i)], p_send.at[j, i], p_recv.at[j, i], sibling
        )

    def x_copy(d):
        to = lax.rem(x + d, XS)
        cols = pl.ds(pl.multiple_of(to * xcols, xcols), xcols)
        return remote(lp_hbm.at[:, cols], xr.at[x], o_send.at[0, d - 1], o_recv.at[0, d - 1], at_rep(q, to, y))

    def x_wait(d):
        slot = xr.at[lax.rem(x + XS - d, XS)]
        return remote(slot, slot, o_send.at[0, d - 1], o_recv.at[0, d - 1], sibling)

    def y_copy(d):
        to = lax.rem(y + d, YS)
        return remote(ysum.at[to], yr.at[y], o_send.at[1, d - 1], o_recv.at[1, d - 1], at_rep(q, x, to))

    def y_wait(d):
        slot = yr.at[lax.rem(y + YS - d, YS)]
        return remote(slot, slot, o_send.at[1, d - 1], o_recv.at[1, d - 1], sibling)

    z_copy = remote(zs, zr, o_send.at[2, 0], o_recv.at[2, 0], partner)

    def y_back(d):
        piece = ps.at[x, y]
        return remote(
            piece, piece, o_send.at[3, d - 1], o_recv.at[3, d - 1], at_rep(q, x, lax.rem(y + d, YS))
        )

    def y_back_wait(d):
        piece = ps.at[x, lax.rem(y + YS - d, YS)]
        return remote(piece, piece, o_send.at[3, d - 1], o_recv.at[3, d - 1], sibling)

    def x_back(d):
        piece = ps.at[x]
        return remote(
            piece, piece, o_send.at[4, d - 1], o_recv.at[4, d - 1], at_rep(q, lax.rem(x + d, XS), y)
        )

    def x_back_wait(d):
        piece = ps.at[lax.rem(x + XS - d, XS)]
        return remote(piece, piece, o_send.at[4, d - 1], o_recv.at[4, d - 1], sibling)

    @pl.when(x > 1)
    def _():
        answer(at_rep(q, 3 - x, y))

    @pl.when(y > 1)
    def _():
        answer(at_rep(q, x, 3 - y))

    @pl.when(q == 1)
    def _():
        answer(partner)

    @pl.when(c == 0)
    def _():
        answer(sibling)

    load_gain.wait()
    lanes = 128
    pieces = width // lanes

    @pl.loop(0, LOADS)
    def _(b):
        tok_load(b).wait()

        @pl.loop(0, block // ROWS)
        def _(r):
            rows = pl.ds(pl.multiple_of(b * block + r * ROWS, ROWS), ROWS)
            sums = [jnp.zeros((ROWS, lanes), F32) for _ in range(4)]
            for m in range(pieces):
                wide = tok[rows, m * lanes : (m + 1) * lanes].astype(F32)
                sums[m % 4] = sums[m % 4] + wide * wide
            total = jnp.sum((sums[0] + sums[1]) + (sums[2] + sums[3]), axis=1, keepdims=True)
            scale = jnp.broadcast_to(lax.rsqrt(total * (1.0 / width) + EPSILON), (ROWS, lanes))
            inv[rows, :] = scale
            for m in range(pieces):
                cols = slice(m * lanes, (m + 1) * lanes)
                nrm[rows, cols] = (tok[rows, cols].astype(F32) * scale * gain[:, cols]).astype(BF16)

    x_heard = 2 * (1 - x_later) + (x == 1).astype(jnp.int32)
    y_heard = 2 * (1 - y_later) + (y == 1).astype(jnp.int32)
    wait_for(here_sem, x_heard + y_heard + (ZS - 1 - q) + c)

    @pl.when(x == 1)
    def _():
        answer(at_rep(q, 0, y))

    @pl.when(y == 1)
    def _():
        answer(at_rep(q, x, 0))

    @pl.when(x == 0)
    def _():
        for d in range(1, XS):
            pl.semaphore_signal(all_sem, inc=1, device_id=at_rep(q, d, y), device_id_type=MESH)

    @pl.when(y == 0)
    def _():
        for d in range(1, YS):
            pl.semaphore_signal(all_sem, inc=1, device_id=at_rep(q, x, d), device_id_type=MESH)

    for i in range(CHUNKS):
        own_to_sibling(i).start()

    load_kg.wait()
    upper = z // (CHIPS // 2)

    def cols_of(owner, i):
        return pl.ds(pl.multiple_of(owner * shard + i * part, part), part)

    def terms(owner, i):
        got = lax.dot_general(
            nrm[:, cols_of(owner, i)], kg[...], (((0,), (0,)), ((), ())), preferred_element_type=F32
        )
        buf[P0 + owner, rows_of(i), :] = got.astype(BF16)

    @pl.loop(0, STEPS)
    def _(t):
        n, i = t // CHUNKS, t % CHUNKS
        j = (1 - upper) * (CHIPS - 1 - n) + upper * n

        @pl.loop(0, CORES)
        def _(turn):
            terms(2 * j + lax.rem(o + turn, CORES), i)

            @pl.when(turn == 0)
            def _():
                terms_to_sibling(j, i).start()

    wait_for(all_sem, x_later + y_later)
    for d in range(1, XS):
        x_copy(d).start()

    kacc[...] = jnp.zeros_like(kacc)
    load_w.wait()

    def use_rows(a, core, i):
        owner = 2 * a + core
        rows = buf[W0 + owner, rows_of(i), :]
        cols = cols_of(owner, i)
        kacc[...] += jnp.dot(nrm[:, cols], rows, preferred_element_type=F32)
        d_normed = lax.dot_general(kg[...], rows, (((1,), (1,)), ((), ())), preferred_element_type=F32)
        wide = tok[:, cols].astype(F32)
        for m in range(part // lanes):
            here = slice(m * lanes, (m + 1) * lanes)
            got = jnp.sum(d_normed[:, here] * wide[:, here] * inv[...], axis=0, keepdims=True)
            g_own[core, a, pl.ds(i * (part // lanes) + m, 1), :] = got

    def add_terms(j, i, base, from_line):
        rows = rows_of(i)
        terms_to_sibling(j, i).wait_recv()
        own = buf[P0 + 2 * j + c, rows, :].astype(F32) + buf[S0 + j, rows, :].astype(F32)

        @pl.when(from_line)
        def _():
            buf[P0 + 2 * j + c, rows, :] = (own + buf[base + j, rows, :].astype(F32)).astype(BF16)

        @pl.when(jnp.logical_not(from_line))
        def _():
            buf[P0 + 2 * j + c, rows, :] = own.astype(BF16)

    gain_swap = remote(g_own.at[o], g_sib, g_send.at[0], g_recv.at[0], sibling)

    def gain_copy(d):
        to = lax.rem(z + d, CHIPS)
        return remote(g_own.at[c, to], g_z.at[z], g_send.at[d], g_recv.at[d], at_chip(to))

    def gain_wait(d):
        slot = g_z.at[lax.rem(z + CHIPS - d, CHIPS)]
        return remote(slot, slot, g_send.at[d], g_recv.at[d], sibling)

    def gain_out(d):
        sem = CHIPS + d - 1
        return remote(g_fin.at[z, c], g_fin.at[z, c], g_send.at[sem], g_recv.at[sem], at_chip(lax.rem(z + d, CHIPS)))

    def gain_in(d):
        slot, sem = g_fin.at[lax.rem(z + CHIPS - d, CHIPS), c], CHIPS + d - 1
        return remote(slot, slot, g_send.at[sem], g_recv.at[sem], sibling)

    gain_back = remote(g_fin.at[:, c], g_fin.at[:, c], g_send.at[2 * CHIPS - 1], g_recv.at[2 * CHIPS - 1], sibling)
    gain_back_in = remote(g_fin.at[:, o], g_fin.at[:, o], g_send.at[2 * CHIPS - 1], g_recv.at[2 * CHIPS - 1], sibling)

    @pl.loop(0, STEPS)
    def _(s):
        k, i = s // CHUNKS, s % CHUNKS

        @pl.when(s == 2)
        def _():
            load_lp.wait()
            for d in range(1, XS):
                x_wait(d).wait_recv()
            for m in range(YS):
                cols = slice(m * ycols, (m + 1) * ycols)
                ysum[m] = (xr[0, :, cols].astype(F32) + xr[1, :, cols].astype(F32)) + (
                    xr[2, :, cols].astype(F32) + xr[3, :, cols].astype(F32)
                )
            for d in range(1, YS):
                y_copy(d).start()
            yr[y] = ysum[y]

        @pl.when(s == 4)
        def _():
            for d in range(1, YS):
                y_wait(d).wait_recv()
            load_op.wait()
            cols = pl.ds(pl.multiple_of(x * xcols + y * ycols, ycols), ycols)
            total = (yr[0] + yr[1]) + (yr[2] + yr[3])
            zs[...] = (float(XS * YS) * op[:, cols] - total).astype(BF16)
            z_copy.start()

        @pl.when(s == 9)
        def _():
            z_copy.wait_recv()
            ps[x, y] = (zs[...].astype(F32) + zr[...].astype(F32)) * (1.0 / (XS * YS * ZS))
            for d in range(1, YS):
                y_back(d).start()

        @pl.when(s == 10)
        def _():
            for d in range(1, YS):
                y_back_wait(d).wait_recv()
            for d in range(1, XS):
                x_back(d).start()

        @pl.when(s == STEPS - 2)
        def _():
            for d in range(1, XS):
                x_back_wait(d).wait_recv()
            load_mo.wait()
            load_step.wait()
            rate = OUTER_LR * (step_ref[0].astype(F32) + 1.0) / WARM
            for a in range(XS):
                for b in range(YS):
                    cols = slice((a * YS + b) * ycols, (a * YS + b + 1) * ycols)
                    pseudo = ps[a, b]
                    moment = OUTER_MOMENTUM * mo[:, cols] + pseudo
                    mo[:, cols] = moment
                    op[:, cols] = op[:, cols] - rate * (pseudo + OUTER_MOMENTUM * moment)

        @pl.when(s == LAST + 1)
        def _():
            for d in range(1, CHIPS):
                gain_wait(d).wait_recv()
            g_fin[z, c] = (g_z[0] + g_z[1]) + (g_z[2] + g_z[3])
            for d in range(1, CHIPS):
                gain_out(d).start()

        @pl.when(s == STEPS - 1)
        def _():
            for d in range(1, CHIPS):
                gain_in(d).wait_recv()
            gain_back.start()

        @pl.when(jnp.logical_and(has_right, s > 1))
        def _():
            line_copy(s - 2, True).wait_send()

        @pl.when(jnp.logical_and(has_left, s > 1))
        def _():
            line_copy(s - 2, False).wait_send()

        @pl.when(k == CHIPS - 1)
        def _():
            for a in range(CHIPS):
                to_sibling(a, i).wait_send()
                terms_to_sibling(a, i).wait_send()

        @pl.when(s == LAST + 1)
        def _():
            gain_swap.wait_send()
            for d in range(1, XS):
                x_copy(d).wait_send()
                x_back(d).wait_send()
            for d in range(1, YS):
                y_copy(d).wait_send()
                y_back(d).wait_send()
            z_copy.wait_send()

        @pl.when(s == STEPS - 1)
        def _():
            for d in range(1, CHIPS):
                gain_copy(d).wait_send()
                gain_out(d).wait_send()

        @pl.when(k == CHIPS - 1)
        def _():
            rows = rows_of(i)
            terms_to_sibling(z, i).wait_recv()
            wg[rows, :] = buf[P0 + 2 * z + c, rows, :].astype(F32) + buf[S0 + z, rows, :].astype(F32)

        @pl.when(has_left)
        def _():
            line_copy(s, True).wait_recv()

        @pl.when(has_right)
        def _():
            line_copy(s, False).wait_recv()

        left_weights = jnp.logical_and(has_left, k <= z - 1)
        right_weights = jnp.logical_and(has_right, k <= CHIPS - 2 - z)

        @pl.when(left_weights)
        def _():
            to_sibling(z - 1 - k, i).start()

        @pl.when(right_weights)
        def _():
            to_sibling(z + 1 + k, i).start()

        @pl.loop(0, 3 * CORES)
        def _(t):
            source, turn = t // CORES, t % CORES
            is_left, is_right, is_own = source == 0, source == 1, source == 2
            a = z + (1 + k) * (is_right.astype(jnp.int32) - is_left.astype(jnp.int32))
            have = jnp.logical_or(
                jnp.logical_or(jnp.logical_and(is_left, left_weights), jnp.logical_and(is_right, right_weights)),
                jnp.logical_and(is_own, k == 1),
            )

            @pl.when(jnp.logical_and(have, turn == 1))
            def _():
                from_sibling(a, i).wait_recv()

            @pl.when(have)
            def _():
                use_rows(a, lax.rem(c + turn, CORES), i)

        @pl.when(s == LAST - 1)
        def _():
            gain_swap.start()
            kout[...] = kacc[...].astype(BF16)

        later = k + 1

        @pl.loop(0, 2)
        def _(t):
            to_left = t == 1
            j = later * (2 * t - 1) + CHIPS * (1 - 2 * t) + z
            goes = jnp.logical_or(
                jnp.logical_and(jnp.logical_not(to_left), jnp.logical_and(has_right, later > z)),
                jnp.logical_and(to_left, jnp.logical_and(has_left, later > CHIPS - 1 - z)),
            )
            comes = jnp.logical_or(jnp.logical_and(to_left, has_right), jnp.logical_and(jnp.logical_not(to_left), has_left))

            @pl.when(jnp.logical_and(later < CHIPS, goes))
            def _():
                add_terms(j, i, R0 + (L0 - R0) * t, comes)

        @pl.when(s == LAST - 1)
        def _():
            gain_swap.wait_recv()
            g_own[c] = g_own[c] + g_sib[...]
            for d in range(1, CHIPS):
                gain_copy(d).start()
            g_z[z] = g_own[c, z]

        early, late = s < LAST + 2 - CHUNKS, jnp.logical_and(s >= LAST, s < LAST + 2)
        n = s + CHUNKS - (CHUNKS - 2) * late.astype(jnp.int32)
        due = jnp.logical_or(early, late)

        @pl.when(jnp.logical_and(has_right, due))
        def _():
            line_copy(n, True).start()

        @pl.when(jnp.logical_and(has_left, due))
        def _():
            line_copy(n, False).start()

        @pl.when(k == CHIPS - 1)
        def _():
            rows = rows_of(i)

            @pl.when(jnp.logical_and(has_left, has_right))
            def _():
                wg[rows, :] += buf[R0 + z, rows, :].astype(F32) + buf[L0 + z, rows, :].astype(F32)

            @pl.when(jnp.logical_not(jnp.logical_and(has_left, has_right)))
            def _():
                wg[rows, :] += buf[R0 + z + (L0 - R0) * (1 - has_left.astype(jnp.int32)), rows, :].astype(F32)

    gain_back_in.wait_recv()
    gain_back.wait_send()

    @pl.when(has_right)
    def _():
        line_copy(STEPS - 2, True).wait_send()
        line_copy(STEPS - 1, True).wait_send()

    @pl.when(has_left)
    def _():
        line_copy(STEPS - 2, False).wait_send()
        line_copy(STEPS - 1, False).wait_send()


def write_out(*refs):
    count = len(PIECES)
    results, outs, sems = refs[:count], refs[count : 2 * count], refs[-1]
    writes = []
    for result, out, pieces in zip(results, outs, PIECES):
        size = result.shape[0] // pieces
        for i in range(pieces):
            here = pl.ds(i * size, size)
            writes.append(pltpu.make_async_copy(result.at[here], out.at[here], sems.at[len(writes)]))
    for write in writes:
        write.start()
    for write in writes:
        write.wait()


def local(tokens, key_weight, key_grad, norm_gain, outer_params, local_params, momentum, outer_step):
    rows, width = tokens.shape
    _, shard, kw = key_weight.shape
    frag = outer_params.shape[0]
    xcols, ycols = width // XS, width // XS // YS
    lanes = 128
    dma, anywhere = pltpu.SemaphoreType.DMA, pl.BlockSpec(memory_space=pltpu.HBM)
    results = (
        ((rows, kw), BF16),
        ((shard, kw), F32),
        ((CHIPS, CORES, shard // lanes, lanes), F32),
        (outer_params.shape, F32),
        (momentum.shape, F32),
    )
    held = pl.pallas_call(
        kernel,
        out_shape=tuple(pltpu.VMEM(*result) for result in results),
        in_specs=[anywhere] * 8,
        out_specs=(pl.BlockSpec(memory_space=pltpu.VMEM),) * 5,
        scratch_shapes=[
            pltpu.VMEM((rows, width), BF16),
            pltpu.VMEM((rows, width), BF16),
            pltpu.VMEM((rows, kw), BF16),
            pltpu.VMEM((1, width), F32),
            pltpu.VMEM((rows, lanes), F32),
            pltpu.VMEM((SLOTS, shard, kw), BF16),
            pltpu.VMEM((rows, kw), F32),
            pltpu.VMEM((CORES, CHIPS, shard // lanes, lanes), F32),
            pltpu.VMEM((CHIPS, shard // lanes, lanes), F32),
            pltpu.VMEM((CHIPS, shard // lanes, lanes), F32),
            pltpu.VMEM((XS, frag, xcols), BF16),
            pltpu.VMEM((YS, frag, ycols), F32),
            pltpu.VMEM((YS, frag, ycols), F32),
            pltpu.VMEM((frag, ycols), BF16),
            pltpu.VMEM((frag, ycols), BF16),
            pltpu.VMEM((XS, YS, frag, ycols), F32),
            pltpu.SMEM((1,), jnp.int32),
            dma((LOADS,)),
            dma((7,)),
            dma((STEPS,)),
            dma((STEPS,)),
            dma((STEPS,)),
            dma((STEPS,)),
            dma((CHIPS, CHUNKS)),
            dma((CHIPS, CHUNKS)),
            dma((CHIPS, CHUNKS)),
            dma((CHIPS, CHUNKS)),
            dma((2 * CHIPS,)),
            dma((2 * CHIPS,)),
            dma((5, 3)),
            dma((5, 3)),
            pltpu.SemaphoreType.REGULAR,
            pltpu.SemaphoreType.REGULAR,
            pltpu.SemaphoreType.REGULAR,
        ],
        compiler_params=pltpu.CompilerParams(
            collective_id=0, has_side_effects=True, vmem_limit_bytes=54 * MIB
        ),
        cost_estimate=pl.CostEstimate(
            flops=6 * rows * width * kw, bytes_accessed=16 * MIB, transcendentals=rows
        ),
        name="outer_and_keys",
    )(
        tokens, key_weight[0], key_grad, norm_gain, outer_params, local_params[0], momentum, outer_step
    )
    keys, weight_grad, gain_grad, new_outer, new_momentum = pl.pallas_call(
        write_out,
        out_shape=tuple(jax.ShapeDtypeStruct(*result) for result in results),
        in_specs=[pl.BlockSpec(memory_space=pltpu.VMEM)] * len(results),
        out_specs=(anywhere,) * len(results),
        scratch_shapes=[dma((sum(PIECES),))],
        compiler_params=pltpu.CompilerParams(vmem_limit_bytes=MIB),
        name="write_out",
    )(*[pltpu.with_memory_space_constraint(a, pltpu.VMEM) for a in held])
    return keys, weight_grad[None], gain_grad.reshape(1, width), new_outer, new_momentum


def solution(mesh):
    placed = (
        P(("rep", "fsdp"), None),
        P("rep", "fsdp", None),
        P(("rep", "fsdp"), None),
        P("rep", None),
        P("fsdp", None),
        P("rep", "fsdp", None),
        P("fsdp", None),
        P(),
    )
    return jax.shard_map(
        local,
        mesh=mesh,
        in_specs=placed,
        out_specs=(
            P(("rep", "fsdp"), None),
            P("rep", "fsdp", None),
            P("rep", None),
            P("fsdp", None),
            P("fsdp", None),
        ),
        check_vma=False,
    )
```

```python
import functools

import jax
import jax.numpy as jnp
from jax import lax
from jax.experimental import pallas as pl
from jax.experimental.pallas import tpu as pltpu
from jax.sharding import PartitionSpec as P

MESH = pl.DeviceIdType.MESH
BF16, F32 = jnp.bfloat16, jnp.float32

WARM = 8
EPSILON = 1e-05
OUTER_LR = 0.7
OUTER_MOMENTUM = 0.9

CHIPS, CORES = 4, 2
XS, YS, ZS = 4, 4, 2
CHUNKS = 4
STEPS = CHIPS * CHUNKS
LAST = STEPS - CHUNKS
LOADS = 6
ROWS = 16
PIECES = (1, 1, 1, 1, 1)
MIB = 1024 * 1024

W0, P0, S0, R0, L0 = 0, 8, 16, 20, 24
SLOTS = 28


def kernel(
    tok_hbm, kw_hbm, kg_hbm, gain_hbm, op_hbm, lp_hbm, mo_hbm, step_hbm,
    kout, wg, g_fin, op, mo,
    tok, nrm, kg, gain, inv, buf, kacc,
    g_own, g_sib, g_z,
    xr, ysum, yr, zs, zr, ps,
    step_ref, tok_sem, ld_sem,
    r_send, r_recv, l_send, l_recv,
    w_send, w_recv, p_send, p_recv,
    g_send, g_recv, o_send, o_recv, here_sem, line_sem, all_sem,
):
    tokens, width = tok.shape
    shard, kw = buf.shape[1:]
    part = shard // CHUNKS
    frag = op.shape[0]
    xcols, ycols = width // XS, width // XS // YS

    rep, fsdp = lax.axis_index("rep"), lax.axis_index("fsdp")
    q, x, y = rep // (XS * YS), (rep // YS) % XS, rep % YS
    z, c = fsdp // CORES, fsdp % CORES
    o = 1 - c

    def at_rep(q_, x_, y_):
        return ((q_ * XS + x_) * YS + y_, fsdp)

    def at_chip(z_):
        return (rep, z_ * CORES + c)

    sibling = (rep, z * CORES + o)
    right, left = at_chip(lax.rem(z + 1, CHIPS)), at_chip(lax.rem(z + CHIPS - 1, CHIPS))
    has_right, has_left = z < CHIPS - 1, z > 0

    def remote(src, dst, send, recv, device):
        return pltpu.make_async_remote_copy(
            src_ref=src, dst_ref=dst, send_sem=send, recv_sem=recv, device_id=device, device_id_type=MESH
        )

    def rows_of(i):
        return pl.ds(pl.multiple_of(i * part, part), part)

    barrier = pltpu.get_barrier_semaphore()
    partner = at_rep(1 - q, x, y)

    def greet(peer):
        pl.semaphore_signal(barrier, inc=1, device_id=peer, device_id_type=MESH)

    def answer(peer):
        pl.semaphore_signal(here_sem, inc=1, device_id=peer, device_id_type=MESH)

    def wait_for(sem, count):
        @pl.when(count > 0)
        def _():
            pl.semaphore_wait(sem, count)

    both = jnp.logical_and(has_right, q == 1)

    @pl.when(q == 0)
    def _():
        greet(partner)

    @pl.when(has_right)
    def _():
        greet(right)

    @pl.when(jnp.logical_and(has_left, q == 1))
    def _():
        greet(left)

    @pl.when(c == 1)
    def _():
        greet(sibling)

    @pl.when(x == 0)
    def _():
        for d in range(1, XS):
            greet(at_rep(q, d, y))

    @pl.when(y == 0)
    def _():
        for d in range(1, YS):
            greet(at_rep(q, x, d))

    x_later, y_later = (x > 0).astype(jnp.int32), (y > 0).astype(jnp.int32)
    wait_for(barrier, has_left.astype(jnp.int32) + both.astype(jnp.int32) + o + x_later + y_later + q)

    @pl.when(jnp.logical_and(has_left, q == 0))
    def _():
        pl.semaphore_signal(line_sem, inc=1, device_id=left, device_id_type=MESH)

    block = tokens // LOADS

    def tok_load(b):
        rows = pl.ds(pl.multiple_of(b * block, block), block)
        return pltpu.make_async_copy(tok_hbm.at[rows], tok.at[rows], tok_sem.at[b])

    load_gain = pltpu.make_async_copy(gain_hbm, gain, ld_sem.at[0])
    load_kg = pltpu.make_async_copy(kg_hbm, kg, ld_sem.at[1])
    load_w = pltpu.make_async_copy(kw_hbm, buf.at[W0 + 2 * z + c], ld_sem.at[2])
    own_x = pl.ds(pl.multiple_of(x * xcols, xcols), xcols)
    load_lp = pltpu.make_async_copy(lp_hbm.at[:, own_x], xr.at[x], ld_sem.at[3])
    load_op = pltpu.make_async_copy(op_hbm, op, ld_sem.at[4])
    load_mo = pltpu.make_async_copy(mo_hbm, mo, ld_sem.at[5])
    load_step = pltpu.make_async_copy(step_hbm, step_ref, ld_sem.at[6])

    def line_first(n, rightward):
        rows = rows_of(n)
        dst = buf.at[W0 + 2 * z + c, rows]
        if rightward:
            return remote(kw_hbm.at[rows], dst, r_send.at[n], r_recv.at[n], right)
        return remote(kw_hbm.at[rows], dst, l_send.at[n], l_recv.at[n], left)

    def line_copy(n, rightward):
        k, rows = n // CHUNKS, rows_of(n % CHUNKS)
        if rightward:
            is_sum = (k - z + CHIPS - 1) // CHIPS
            weight, owner = 2 * (z - k) + c, CHIPS + z - k
            src = (1 - is_sum) * (W0 + weight) + is_sum * (P0 + 2 * owner + c)
            dst = (1 - is_sum) * (W0 + weight) + is_sum * (R0 + owner)
            return remote(buf.at[src, rows], buf.at[dst, rows], r_send.at[n], r_recv.at[n], right)
        is_sum = (k + z) // CHIPS
        weight, owner = 2 * (z + k) + c, k + z - CHIPS
        src = (1 - is_sum) * (W0 + weight) + is_sum * (P0 + 2 * owner + c)
        dst = (1 - is_sum) * (W0 + weight) + is_sum * (L0 + owner)
        return remote(buf.at[src, rows], buf.at[dst, rows], l_send.at[n], l_recv.at[n], left)

    @pl.when(has_left)
    def _():
        for n in range(CHUNKS):
            line_first(n, False).start()

    @pl.when(jnp.logical_and(has_right, q == 0))
    def _():
        pl.semaphore_wait(line_sem, 1)

    @pl.when(has_right)
    def _():
        for n in range(CHUNKS):
            line_first(n, True).start()

    load_gain.start()
    tok_load(0).start()
    load_kg.start()
    for b in range(1, LOADS):
        tok_load(b).start()
    for load in (load_w, load_lp, load_op, load_mo, load_step):
        load.start()

    def own_to_sibling(i):
        rows = rows_of(i)
        return remote(
            kw_hbm.at[rows], buf.at[W0 + 2 * z + c, rows], w_send.at[z, i], w_recv.at[z, i], sibling
        )

    def to_sibling(a, i):
        there = buf.at[W0 + 2 * a + c, rows_of(i)]
        return remote(there, there, w_send.at[a, i], w_recv.at[a, i], sibling)

    def from_sibling(a, i):
        there = buf.at[W0 + 2 * a + o, rows_of(i)]
        return remote(there, there, w_send.at[a, i], w_recv.at[a, i], sibling)

    def terms_to_sibling(j, i):
        return remote(
            buf.at[P0 + 2 * j + o, rows_of(i)], buf.at[S0 + j, rows_of(i)], p_send.at[j, i], p_recv.at[j, i], sibling
        )

    def x_copy(d):
        to = lax.rem(x + d, XS)
        cols = pl.ds(pl.multiple_of(to * xcols, xcols), xcols)
        return remote(lp_hbm.at[:, cols], xr.at[x], o_send.at[0, d - 1], o_recv.at[0, d - 1], at_rep(q, to, y))

    def x_wait(d):
        slot = xr.at[lax.rem(x + XS - d, XS)]
        return remote(slot, slot, o_send.at[0, d - 1], o_recv.at[0, d - 1], sibling)

    def y_copy(d):
        to = lax.rem(y + d, YS)
        return remote(ysum.at[to], yr.at[y], o_send.at[1, d - 1], o_recv.at[1, d - 1], at_rep(q, x, to))

    def y_wait(d):
        slot = yr.at[lax.rem(y + YS - d, YS)]
        return remote(slot, slot, o_send.at[1, d - 1], o_recv.at[1, d - 1], sibling)

    z_copy = remote(zs, zr, o_send.at[2, 0], o_recv.at[2, 0], partner)

    def y_back(d):
        piece = ps.at[x, y]
        return remote(
            piece, piece, o_send.at[3, d - 1], o_recv.at[3, d - 1], at_rep(q, x, lax.rem(y + d, YS))
        )

    def y_back_wait(d):
        piece = ps.at[x, lax.rem(y + YS - d, YS)]
        return remote(piece, piece, o_send.at[3, d - 1], o_recv.at[3, d - 1], sibling)

    def x_back(d):
        piece = ps.at[x]
        return remote(
            piece, piece, o_send.at[4, d - 1], o_recv.at[4, d - 1], at_rep(q, lax.rem(x + d, XS), y)
        )

    def x_back_wait(d):
        piece = ps.at[lax.rem(x + XS - d, XS)]
        return remote(piece, piece, o_send.at[4, d - 1], o_recv.at[4, d - 1], sibling)

    @pl.when(x > 0)
    def _():
        answer(at_rep(q, 0, y))

    @pl.when(y > 0)
    def _():
        answer(at_rep(q, x, 0))

    @pl.when(q == 1)
    def _():
        answer(partner)

    @pl.when(c == 0)
    def _():
        answer(sibling)

    load_gain.wait()
    lanes = 128
    pieces = width // lanes

    @pl.loop(0, LOADS)
    def _(b):
        tok_load(b).wait()

        @pl.loop(0, block // ROWS)
        def _(r):
            rows = pl.ds(pl.multiple_of(b * block + r * ROWS, ROWS), ROWS)
            sums = [jnp.zeros((ROWS, lanes), F32) for _ in range(4)]
            for m in range(pieces):
                wide = tok[rows, m * lanes : (m + 1) * lanes].astype(F32)
                sums[m % 4] = sums[m % 4] + wide * wide
            total = jnp.sum((sums[0] + sums[1]) + (sums[2] + sums[3]), axis=1, keepdims=True)
            scale = jnp.broadcast_to(lax.rsqrt(total * (1.0 / width) + EPSILON), (ROWS, lanes))
            inv[rows, :] = scale
            for m in range(pieces):
                cols = slice(m * lanes, (m + 1) * lanes)
                nrm[rows, cols] = (tok[rows, cols].astype(F32) * scale * gain[:, cols]).astype(BF16)

    wait_for(here_sem, (1 - x_later) * (XS - 1) + (1 - y_later) * (YS - 1) + (ZS - 1 - q) + c)

    @pl.when(x == 0)
    def _():
        for d in range(1, XS):
            pl.semaphore_signal(all_sem, inc=1, device_id=at_rep(q, d, y), device_id_type=MESH)

    @pl.when(y == 0)
    def _():
        for d in range(1, YS):
            pl.semaphore_signal(all_sem, inc=1, device_id=at_rep(q, x, d), device_id_type=MESH)

    for i in range(CHUNKS):
        own_to_sibling(i).start()

    load_kg.wait()
    upper = z // (CHIPS // 2)

    def cols_of(owner, i):
        return pl.ds(pl.multiple_of(owner * shard + i * part, part), part)

    def terms(owner, i):
        got = lax.dot_general(
            nrm[:, cols_of(owner, i)], kg[...], (((0,), (0,)), ((), ())), preferred_element_type=F32
        )
        buf[P0 + owner, rows_of(i), :] = got.astype(BF16)

    @pl.loop(0, STEPS)
    def _(t):
        n, i = t // CHUNKS, t % CHUNKS
        j = (1 - upper) * (CHIPS - 1 - n) + upper * n

        @pl.loop(0, CORES)
        def _(turn):
            terms(2 * j + lax.rem(o + turn, CORES), i)

            @pl.when(turn == 0)
            def _():
                terms_to_sibling(j, i).start()

    wait_for(all_sem, x_later + y_later)
    for d in range(1, XS):
        x_copy(d).start()

    kacc[...] = jnp.zeros_like(kacc)
    load_w.wait()

    def use_rows(a, core, i):
        owner = 2 * a + core
        rows = buf[W0 + owner, rows_of(i), :]
        cols = cols_of(owner, i)
        kacc[...] += jnp.dot(nrm[:, cols], rows, preferred_element_type=F32)
        d_normed = lax.dot_general(kg[...], rows, (((1,), (1,)), ((), ())), preferred_element_type=F32)
        wide = tok[:, cols].astype(F32)
        for m in range(part // lanes):
            here = slice(m * lanes, (m + 1) * lanes)
            got = jnp.sum(d_normed[:, here] * wide[:, here] * inv[...], axis=0, keepdims=True)
            g_own[core, a, pl.ds(i * (part // lanes) + m, 1), :] = got

    def add_terms(j, i, base, from_line):
        rows = rows_of(i)
        terms_to_sibling(j, i).wait_recv()
        own = buf[P0 + 2 * j + c, rows, :].astype(F32) + buf[S0 + j, rows, :].astype(F32)

        @pl.when(from_line)
        def _():
            buf[P0 + 2 * j + c, rows, :] = (own + buf[base + j, rows, :].astype(F32)).astype(BF16)

        @pl.when(jnp.logical_not(from_line))
        def _():
            buf[P0 + 2 * j + c, rows, :] = own.astype(BF16)

    gain_swap = remote(g_own.at[o], g_sib, g_send.at[0], g_recv.at[0], sibling)

    def gain_copy(d):
        return remote(g_z.at[z], g_z.at[z], g_send.at[d], g_recv.at[d], at_chip(lax.rem(z + d, CHIPS)))

    def gain_wait(d):
        slot = g_z.at[lax.rem(z + CHIPS - d, CHIPS)]
        return remote(slot, slot, g_send.at[d], g_recv.at[d], sibling)

    gain_back = remote(g_fin.at[:, c], g_fin.at[:, c], g_send.at[CHIPS], g_recv.at[CHIPS], sibling)
    gain_back_in = remote(g_fin.at[:, o], g_fin.at[:, o], g_send.at[CHIPS], g_recv.at[CHIPS], sibling)

    @pl.loop(0, STEPS)
    def _(s):
        k, i = s // CHUNKS, s % CHUNKS

        @pl.when(s == 2)
        def _():
            load_lp.wait()
            for d in range(1, XS):
                x_wait(d).wait_recv()
            for m in range(YS):
                cols = slice(m * ycols, (m + 1) * ycols)
                ysum[m] = (xr[0, :, cols].astype(F32) + xr[1, :, cols].astype(F32)) + (
                    xr[2, :, cols].astype(F32) + xr[3, :, cols].astype(F32)
                )
            for d in range(1, YS):
                y_copy(d).start()
            yr[y] = ysum[y]

        @pl.when(s == 4)
        def _():
            for d in range(1, YS):
                y_wait(d).wait_recv()
            load_op.wait()
            cols = pl.ds(pl.multiple_of(x * xcols + y * ycols, ycols), ycols)
            total = (yr[0] + yr[1]) + (yr[2] + yr[3])
            zs[...] = (float(XS * YS) * op[:, cols] - total).astype(BF16)
            z_copy.start()

        @pl.when(s == 9)
        def _():
            z_copy.wait_recv()
            ps[x, y] = (zs[...].astype(F32) + zr[...].astype(F32)) * (1.0 / (XS * YS * ZS))
            for d in range(1, YS):
                y_back(d).start()

        @pl.when(s == 10)
        def _():
            for d in range(1, YS):
                y_back_wait(d).wait_recv()
            for d in range(1, XS):
                x_back(d).start()

        @pl.when(s == STEPS - 2)
        def _():
            for d in range(1, XS):
                x_back_wait(d).wait_recv()
            load_mo.wait()
            load_step.wait()
            rate = OUTER_LR * (step_ref[0].astype(F32) + 1.0) / WARM
            for a in range(XS):
                for b in range(YS):
                    cols = slice((a * YS + b) * ycols, (a * YS + b + 1) * ycols)
                    pseudo = ps[a, b]
                    moment = OUTER_MOMENTUM * mo[:, cols] + pseudo
                    mo[:, cols] = moment
                    op[:, cols] = op[:, cols] - rate * (pseudo + OUTER_MOMENTUM * moment)

        @pl.when(s == STEPS - 1)
        def _():
            for d in range(1, CHIPS):
                gain_wait(d).wait_recv()
            total = (g_z[0].astype(F32) + g_z[1].astype(F32)) + (g_z[2].astype(F32) + g_z[3].astype(F32))
            size = total.shape[0] // CHIPS
            for j in range(CHIPS):
                g_fin[j, c] = total[j * size : (j + 1) * size]
            gain_back.start()

        @pl.when(jnp.logical_and(has_right, s > 1))
        def _():
            line_copy(s - 2, True).wait_send()

        @pl.when(jnp.logical_and(has_left, s > 1))
        def _():
            line_copy(s - 2, False).wait_send()

        @pl.when(k == CHIPS - 1)
        def _():
            for a in range(CHIPS):
                to_sibling(a, i).wait_send()
                terms_to_sibling(a, i).wait_send()

        @pl.when(s == LAST + 1)
        def _():
            gain_swap.wait_send()
            for d in range(1, XS):
                x_copy(d).wait_send()
                x_back(d).wait_send()
            for d in range(1, YS):
                y_copy(d).wait_send()
                y_back(d).wait_send()
            z_copy.wait_send()

        @pl.when(s == STEPS - 1)
        def _():
            for d in range(1, CHIPS):
                gain_copy(d).wait_send()

        @pl.when(k == CHIPS - 1)
        def _():
            rows = rows_of(i)
            terms_to_sibling(z, i).wait_recv()
            wg[rows, :] = buf[P0 + 2 * z + c, rows, :].astype(F32) + buf[S0 + z, rows, :].astype(F32)

        @pl.when(has_left)
        def _():
            line_copy(s, True).wait_recv()

        @pl.when(has_right)
        def _():
            line_copy(s, False).wait_recv()

        left_weights = jnp.logical_and(has_left, k <= z - 1)
        right_weights = jnp.logical_and(has_right, k <= CHIPS - 2 - z)

        @pl.when(left_weights)
        def _():
            to_sibling(z - 1 - k, i).start()

        @pl.when(right_weights)
        def _():
            to_sibling(z + 1 + k, i).start()

        @pl.loop(0, 3 * CORES)
        def _(t):
            source, turn = t // CORES, t % CORES
            is_left, is_right, is_own = source == 0, source == 1, source == 2
            a = z + (1 + k) * (is_right.astype(jnp.int32) - is_left.astype(jnp.int32))
            have = jnp.logical_or(
                jnp.logical_or(jnp.logical_and(is_left, left_weights), jnp.logical_and(is_right, right_weights)),
                jnp.logical_and(is_own, k == 1),
            )

            @pl.when(jnp.logical_and(have, turn == 1))
            def _():
                from_sibling(a, i).wait_recv()

            @pl.when(have)
            def _():
                use_rows(a, lax.rem(c + turn, CORES), i)

        @pl.when(s == LAST - 1)
        def _():
            gain_swap.start()
            kout[...] = kacc[...].astype(BF16)

        later = k + 1

        @pl.loop(0, 2)
        def _(t):
            to_left = t == 1
            j = later * (2 * t - 1) + CHIPS * (1 - 2 * t) + z
            goes = jnp.logical_or(
                jnp.logical_and(jnp.logical_not(to_left), jnp.logical_and(has_right, later > z)),
                jnp.logical_and(to_left, jnp.logical_and(has_left, later > CHIPS - 1 - z)),
            )
            comes = jnp.logical_or(jnp.logical_and(to_left, has_right), jnp.logical_and(jnp.logical_not(to_left), has_left))

            @pl.when(jnp.logical_and(later < CHIPS, goes))
            def _():
                add_terms(j, i, R0 + (L0 - R0) * t, comes)

        @pl.when(s == LAST - 1)
        def _():
            gain_swap.wait_recv()
            g_z[z] = (g_own[c] + g_sib[...]).reshape(g_z.shape[1:]).astype(BF16)
            for d in range(1, CHIPS):
                gain_copy(d).start()

        early, late = s < LAST + 2 - CHUNKS, jnp.logical_and(s >= LAST - 1, s <= LAST)
        n = s + CHUNKS - late.astype(jnp.int32)
        due = jnp.logical_or(early, late)

        @pl.when(jnp.logical_and(has_right, due))
        def _():
            line_copy(n, True).start()

        @pl.when(jnp.logical_and(has_left, due))
        def _():
            line_copy(n, False).start()

        @pl.when(k == CHIPS - 1)
        def _():
            rows = rows_of(i)

            @pl.when(jnp.logical_and(has_left, has_right))
            def _():
                wg[rows, :] += buf[R0 + z, rows, :].astype(F32) + buf[L0 + z, rows, :].astype(F32)

            @pl.when(jnp.logical_not(jnp.logical_and(has_left, has_right)))
            def _():
                wg[rows, :] += buf[R0 + z + (L0 - R0) * (1 - has_left.astype(jnp.int32)), rows, :].astype(F32)

    gain_back_in.wait_recv()
    gain_back.wait_send()

    @pl.when(has_right)
    def _():
        line_copy(STEPS - 2, True).wait_send()
        line_copy(STEPS - 1, True).wait_send()

    @pl.when(has_left)
    def _():
        line_copy(STEPS - 2, False).wait_send()
        line_copy(STEPS - 1, False).wait_send()


def write_out(*refs):
    count = len(PIECES)
    results, outs, sems = refs[:count], refs[count : 2 * count], refs[-1]
    writes = []
    for result, out, pieces in zip(results, outs, PIECES):
        size = result.shape[0] // pieces
        for i in range(pieces):
            here = pl.ds(i * size, size)
            writes.append(pltpu.make_async_copy(result.at[here], out.at[here], sems.at[len(writes)]))
    for write in writes:
        write.start()
    for write in writes:
        write.wait()


def local(tokens, key_weight, key_grad, norm_gain, outer_params, local_params, momentum, outer_step):
    rows, width = tokens.shape
    _, shard, kw = key_weight.shape
    frag = outer_params.shape[0]
    xcols, ycols = width // XS, width // XS // YS
    lanes = 128
    dma, anywhere = pltpu.SemaphoreType.DMA, pl.BlockSpec(memory_space=pltpu.HBM)
    results = (
        ((rows, kw), BF16),
        ((shard, kw), F32),
        ((CHIPS, CORES, shard // lanes, lanes), F32),
        (outer_params.shape, F32),
        (momentum.shape, F32),
    )
    held = pl.pallas_call(
        kernel,
        out_shape=tuple(pltpu.VMEM(*result) for result in results),
        in_specs=[anywhere] * 8,
        out_specs=(pl.BlockSpec(memory_space=pltpu.VMEM),) * 5,
        scratch_shapes=[
            pltpu.VMEM((rows, width), BF16),
            pltpu.VMEM((rows, width), BF16),
            pltpu.VMEM((rows, kw), BF16),
            pltpu.VMEM((1, width), F32),
            pltpu.VMEM((rows, lanes), F32),
            pltpu.VMEM((SLOTS, shard, kw), BF16),
            pltpu.VMEM((rows, kw), F32),
            pltpu.VMEM((CORES, CHIPS, shard // lanes, lanes), F32),
            pltpu.VMEM((CHIPS, shard // lanes, lanes), F32),
            pltpu.VMEM((CHIPS, width // CORES // lanes, lanes), BF16),
            pltpu.VMEM((XS, frag, xcols), BF16),
            pltpu.VMEM((YS, frag, ycols), F32),
            pltpu.VMEM((YS, frag, ycols), F32),
            pltpu.VMEM((frag, ycols), BF16),
            pltpu.VMEM((frag, ycols), BF16),
            pltpu.VMEM((XS, YS, frag, ycols), F32),
            pltpu.SMEM((1,), jnp.int32),
            dma((LOADS,)),
            dma((7,)),
            dma((STEPS,)),
            dma((STEPS,)),
            dma((STEPS,)),
            dma((STEPS,)),
            dma((CHIPS, CHUNKS)),
            dma((CHIPS, CHUNKS)),
            dma((CHIPS, CHUNKS)),
            dma((CHIPS, CHUNKS)),
            dma((CHIPS + 1,)),
            dma((CHIPS + 1,)),
            dma((5, 3)),
            dma((5, 3)),
            pltpu.SemaphoreType.REGULAR,
            pltpu.SemaphoreType.REGULAR,
            pltpu.SemaphoreType.REGULAR,
        ],
        compiler_params=pltpu.CompilerParams(
            collective_id=0, has_side_effects=True, vmem_limit_bytes=54 * MIB
        ),
        cost_estimate=pl.CostEstimate(
            flops=6 * rows * width * kw, bytes_accessed=16 * MIB, transcendentals=rows
        ),
        name="outer_and_keys",
    )(
        tokens, key_weight[0], key_grad, norm_gain, outer_params, local_params[0], momentum, outer_step
    )
    keys, weight_grad, gain_grad, new_outer, new_momentum = pl.pallas_call(
        write_out,
        out_shape=tuple(jax.ShapeDtypeStruct(*result) for result in results),
        in_specs=[pl.BlockSpec(memory_space=pltpu.VMEM)] * len(results),
        out_specs=(anywhere,) * len(results),
        scratch_shapes=[dma((sum(PIECES),))],
        compiler_params=pltpu.CompilerParams(vmem_limit_bytes=MIB),
        name="write_out",
    )(*[pltpu.with_memory_space_constraint(a, pltpu.VMEM) for a in held])
    return keys, weight_grad[None], gain_grad.reshape(1, width), new_outer, new_momentum


def solution(mesh):
    placed = (
        P(("rep", "fsdp"), None),
        P("rep", "fsdp", None),
        P(("rep", "fsdp"), None),
        P("rep", None),
        P("fsdp", None),
        P("rep", "fsdp", None),
        P("fsdp", None),
        P(),
    )
    return jax.shard_map(
        local,
        mesh=mesh,
        in_specs=placed,
        out_specs=(
            P(("rep", "fsdp"), None),
            P("rep", "fsdp", None),
            P("rep", None),
            P("fsdp", None),
            P("fsdp", None),
        ),
        check_vma=False,
    )
```
